256 devices in a mesh: gx: 4 (over x), gy: 8 (over z_lo, core), gz: 8 (over z_hi, y).
Axes of the slice: x: 4, y: 4, z: 8 (z_hi: 2, z_lo: 4; z = z_hi * 4 + z_lo), core: 2. Of those that a mesh axis runs over, the one named last changes fastest.
Arguments:
- populations: float32 [1024, 19, 4096], P(('gx', 'gy', 'gz')), as said below
- neighbours: int32 [1024, 6], P(('gx', 'gy', 'gz')), may hold values from -1 to 1023, as said below
- substeps: int32 [1024], P(('gx', 'gy', 'gz')), may hold values from 1 to 4
- moves: int32 [256, 2], P(('gx', 'gy', 'gz')), may hold values from 0 to 3, as said below
Outputs:
- new_populations: float32 [1024, 19, 4096], P(('gx', 'gy', 'gz'))
- block_ids: int32 [1024], P(('gx', 'gy', 'gz'))
The draws below stay inside these ranges and needn't reach their ends.
Inputs may be any that keep to these rules, and one draw needn't show every extreme that they name: `neighbours`: each entry is -1 or a block whose index differs from the block's own by at most 4. `moves`: each row holds 2 different slots. `populations`: every population is positive.
All inputs are finite; a program needn't handle non-finite values.
Results may differ from the reference program's by a relative error of at most 0.0003.
Values sent between devices are 32-bit elements; how exact they have to be, the bound alone decides.
A program may use at most 128 MiB of HBM per device.

```python
import jax
import jax.numpy as jnp
import numpy as np
from jax import lax

BE = 16
SMAX = 4
BLK_DEV = 4
MOVE = 2
CELLS = 4096
NBLOCKS = 1024
N_GY = 8
N_GZ = 8


LATTICE_WEIGHTS = np.array([1.0 / 3.0] + [1.0 / 18.0] * 6 + [1.0 / 36.0] * 12, np.float32)


def draw_populations(key, part):
    factor = jax.random.uniform(key, (NBLOCKS, 19, CELLS), jnp.float32, 0.5, 1.5)
    return factor * jnp.asarray(LATTICE_WEIGHTS)[None, :, None]


def shared_plan(key):
    device_count = NBLOCKS // BLK_DEV
    first, second, third, fourth = jax.random.split(jax.random.fold_in(key, 17), 4)
    scores = jax.random.randint(first, (device_count, BLK_DEV), 0, 1 << 20) * BLK_DEV + jnp.arange(BLK_DEV)[None, :]
    order = jnp.argsort(scores, axis=1).astype(jnp.int32)
    ranks = jnp.argsort(order, axis=1)
    heavy = jax.random.randint(second, (device_count,), 0, 4) == 0
    forced = jax.random.randint(third, (), 0, device_count)
    heavy = heavy | (jnp.arange(device_count) == forced)
    light = jnp.where(ranks < MOVE, jax.random.randint(fourth, (device_count, BLK_DEV), 1, 3), 1)
    counts = jnp.where(heavy[:, None], SMAX, light).astype(jnp.int32)
    return (order[:, :MOVE], counts.reshape(NBLOCKS))


def draw_substeps(key, part):
    return shared_plan(key)[1]


def draw_moves(key, part):
    return shared_plan(key)[0]


def draw_neighbours(key, part):
    first, second = jax.random.split(jax.random.fold_in(key, 5))
    own = jnp.arange(NBLOCKS, dtype=jnp.int32)[:, None]
    offsets = jax.random.randint(first, (NBLOCKS, 6), -BLK_DEV, BLK_DEV + 1)
    candidate = own + offsets
    walled = jax.random.randint(second, (NBLOCKS, 6), 0, 6) == 0
    valid = (candidate >= 0) & (candidate < NBLOCKS) & ~walled
    result = jnp.where(valid, candidate, -1).astype(jnp.int32)
    result = result.at[0, 0].set(-1)
    result = result.at[NBLOCKS - 2, 1].set(NBLOCKS - 1)
    return result


def setup_inputs(seed: int = 0) -> dict:
    key_list = jax.random.split(jax.random.key(seed), 5)
    populations = draw_populations(jax.random.fold_in(key_list[4], 71), 0)
    neighbours = draw_neighbours(jax.random.fold_in(key_list[4], 71), 0)
    substeps = draw_substeps(jax.random.fold_in(key_list[4], 71), 0)
    moves = draw_moves(jax.random.fold_in(key_list[4], 71), 0)
    return {"populations": populations, "neighbours": neighbours, "substeps": substeps, "moves": moves}


VELOCITY = np.array([[0, 0, 0], [1, 0, 0], [-1, 0, 0], [0, 1, 0], [0, -1, 0], [0, 0, 1], [0, 0, -1],
                     [1, 1, 0], [-1, -1, 0], [1, -1, 0], [-1, 1, 0], [1, 0, 1], [-1, 0, -1],
                     [1, 0, -1], [-1, 0, 1], [0, 1, 1], [0, -1, -1], [0, 1, -1], [0, -1, 1]], np.int32)
OPPOSITE = np.array([0, 2, 1, 4, 3, 6, 5, 8, 7, 10, 9, 12, 11, 14, 13, 16, 15, 18, 17], np.int32)
FACE_DIRECTIONS = np.array([[2, 8, 10, 12, 14], [1, 7, 9, 11, 13], [4, 8, 9, 16, 18],
                            [3, 7, 10, 15, 17], [6, 12, 13, 16, 17], [5, 11, 14, 15, 18]], np.int32)
FACE_PARTNER = np.array([1, 0, 3, 2, 5, 4], np.int32)
RELAX_FIXED = np.array([0, 1.19, 1.4, 0, 1.2, 0, 1.2, 0, 1.2, 0, 1.4, 0, 1.4, 0, 0, 0, 1.98, 1.98, 1.98], np.float32)
SHEAR_ROWS = np.array([0, 0, 0, 0, 0, 0, 0, 0, 0, 1, 0, 1, 0, 1, 1, 1, 0, 0, 0], np.float32)
BASE_RATE = 1.6


def moment_table():
    vel_x, vel_y, vel_z = [VELOCITY[:, k].astype(np.float32) for k in range(3)]
    speed_sq = vel_x ** 2 + vel_y ** 2 + vel_z ** 2
    moment_list = [np.ones(19, np.float32), 19 * speed_sq - 30, (21 * speed_sq ** 2 - 53 * speed_sq + 24) / 2,
                   vel_x, (5 * speed_sq - 9) * vel_x, vel_y, (5 * speed_sq - 9) * vel_y,
                   vel_z, (5 * speed_sq - 9) * vel_z, 3 * vel_x ** 2 - speed_sq,
                   (3 * speed_sq - 5) * (3 * vel_x ** 2 - speed_sq), vel_y ** 2 - vel_z ** 2,
                   (3 * speed_sq - 5) * (vel_y ** 2 - vel_z ** 2), vel_x * vel_y, vel_y * vel_z,
                   vel_x * vel_z, (vel_y ** 2 - vel_z ** 2) * vel_x, (vel_z ** 2 - vel_x ** 2) * vel_y,
                   (vel_x ** 2 - vel_y ** 2) * vel_z]
    return np.stack(moment_list).astype(np.float32)


def inverse_table():
    table = moment_table()
    return (table.T / (table ** 2).sum(1)).astype(np.float32)


def build_masks(block_edge):
    flat = np.arange(block_edge ** 3, dtype=np.int32)
    positions = np.stack([flat // (block_edge * block_edge), (flat // block_edge) % block_edge, flat % block_edge])
    result = np.zeros((6, 19, block_edge ** 3), np.int32)
    for which in range(19):
        source = positions - VELOCITY[which][:, None]
        settled = np.zeros(block_edge ** 3, bool)
        for axis_num in range(3):
            below = (source[axis_num] < 0) & ~settled
            beyond = (source[axis_num] > block_edge - 1) & ~settled
            result[2 * axis_num, which, below] = 1
            result[2 * axis_num + 1, which, beyond] = 1
            settled = settled | below | beyond
    return result


def face_pack(state):
    block_cube = state.reshape(19, BE, BE, BE)
    faces = [block_cube[:, 0], block_cube[:, BE - 1], block_cube[:, :, 0], block_cube[:, :, BE - 1],
             block_cube[:, :, :, 0], block_cube[:, :, :, BE - 1]]
    return jnp.stack([faces[face][FACE_DIRECTIONS[face]].reshape(5, BE * BE) for face in range(6)])


def collide(state, shear_rate):
    moments = jnp.dot(jnp.asarray(moment_table()), state, precision=lax.Precision.HIGHEST)
    density = moments[0]
    flux_x, flux_y, flux_z = moments[3], moments[5], moments[7]
    flux_sq = flux_x * flux_x + flux_y * flux_y + flux_z * flux_z
    stress_xx = 3 * flux_x * flux_x - flux_sq
    stress_ww = flux_y * flux_y - flux_z * flux_z
    zeros = jnp.zeros_like(density)
    balance = jnp.stack([density, -11 * density + 19 * flux_sq, 3 * density - 5.5 * flux_sq,
                         flux_x, -2.0 / 3.0 * flux_x, flux_y, -2.0 / 3.0 * flux_y, flux_z, -2.0 / 3.0 * flux_z,
                         stress_xx, -0.5 * stress_xx, stress_ww, -0.5 * stress_ww,
                         flux_x * flux_y, flux_y * flux_z, flux_x * flux_z, zeros, zeros, zeros])
    relax_rates = RELAX_FIXED[:, None] + SHEAR_ROWS[:, None] * shear_rate
    relaxed = moments - relax_rates * (moments - balance)
    return jnp.dot(jnp.asarray(inverse_table()), relaxed, precision=lax.Precision.HIGHEST)


def face_plane(halo_in, face):
    return jnp.zeros((19, BE, BE), halo_in.dtype).at[FACE_DIRECTIONS[face ^ 1]].set(halo_in[face].reshape(5, BE, BE))


def stream(post, halo_in, wall_faces):
    extended = jnp.pad(post.reshape(19, BE, BE, BE), ((0, 0), (1, 1), (1, 1), (1, 1)))
    extended = extended.at[:, 1:-1, 1:-1, 0].set(face_plane(halo_in, 4))
    extended = extended.at[:, 1:-1, 1:-1, -1].set(face_plane(halo_in, 5))
    extended = extended.at[:, 1:-1, 0, :].set(jnp.pad(face_plane(halo_in, 2), ((0, 0), (0, 0), (1, 1)), mode="edge"))
    extended = extended.at[:, 1:-1, -1, :].set(jnp.pad(face_plane(halo_in, 3), ((0, 0), (0, 0), (1, 1)), mode="edge"))
    extended = extended.at[:, 0, :, :].set(jnp.pad(face_plane(halo_in, 0), ((0, 0), (1, 1), (1, 1)), mode="edge"))
    extended = extended.at[:, -1, :, :].set(jnp.pad(face_plane(halo_in, 1), ((0, 0), (1, 1), (1, 1)), mode="edge"))
    moved = []
    for which in range(19):
        step_x, step_y, step_z = [int(v) for v in VELOCITY[which]]
        moved.append(extended[which, 1 - step_x:1 - step_x + BE, 1 - step_y:1 - step_y + BE, 1 - step_z:1 - step_z + BE])
    read = jnp.stack(moved).reshape(19, BE ** 3)
    bounce = jnp.tensordot(wall_faces, jnp.asarray(build_masks(BE)), axes=1) > 0
    return jnp.where(bounce, post[OPPOSITE], read)


def advance(packed):
    state, halo_in, wall_faces, step_count = packed
    shear_rate = 1.0 / (step_count.astype(jnp.float32) * (1.0 / BASE_RATE - 0.5) + 0.5)

    def cycle(index, current):
        return stream(collide(current, shear_rate), halo_in, wall_faces)

    return lax.fori_loop(0, step_count, cycle, state)


def reference(populations, neighbours, substeps, moves):
    packets = jax.vmap(face_pack)(populations)
    valid = neighbours >= 0
    safe_index = jnp.where(valid, neighbours, 0)
    halo_in = packets[safe_index, jnp.asarray(FACE_PARTNER)[None, :]]
    halo_in = jnp.where(valid[:, :, None, None], halo_in, 0.0)
    wall_faces = (~valid).astype(jnp.int32)
    stepped = lax.map(advance, (populations, halo_in, wall_faces, substeps))
    device_count = NBLOCKS // BLK_DEV
    devices = jnp.arange(device_count, dtype=jnp.int32)
    partner = jnp.bitwise_xor(devices, N_GY * N_GZ)
    targets = devices[:, None] * BLK_DEV + moves
    anchors = partner[:, None] * BLK_DEV + moves[partner]
    source = jnp.arange(NBLOCKS, dtype=jnp.int32).at[targets.reshape(-1)].set(anchors.reshape(-1).astype(jnp.int32))
    return stepped[source], source
```

```python
import functools

import jax
import jax.numpy as jnp
import numpy as np
from jax import lax
from jax.experimental import pallas as pl
from jax.experimental.pallas import tpu as pltpu
from jax.sharding import PartitionSpec as P

MESH = pl.DeviceIdType.MESH
AXES = ("gx", "gy", "gz")
VELOCITY = [
    (0, 0, 0), (1, 0, 0), (-1, 0, 0), (0, 1, 0), (0, -1, 0), (0, 0, 1), (0, 0, -1),
    (1, 1, 0), (-1, -1, 0), (1, -1, 0), (-1, 1, 0), (1, 0, 1), (-1, 0, -1),
    (1, 0, -1), (-1, 0, 1), (0, 1, 1), (0, -1, -1), (0, 1, -1), (0, -1, 1),
]
OPPOSITE = [0, 2, 1, 4, 3, 6, 5, 8, 7, 10, 9, 12, 11, 14, 13, 16, 15, 18, 17]
LEAVING = [
    [2, 8, 10, 12, 14], [1, 7, 9, 11, 13], [4, 8, 9, 16, 18],
    [3, 7, 10, 15, 17], [6, 12, 13, 16, 17], [5, 11, 14, 15, 18],
]
COUNT_ROW, SLOT_ROW, Y_ROW, Z_ROW, SENT_ROWS, PACKET_ROWS = 20, 21, 24, 56, 88, 96
TOP = 8


def turned(value, by):
    by = by % 128
    return value if by == 0 else pltpu.roll(value, by, 1)


def grid_iotas():
    row = lax.broadcasted_iota(jnp.int32, (8, 128), 0)
    lane = lax.broadcasted_iota(jnp.int32, (8, 128), 1)
    return row, lane


def unpacked(raw, cube, block):
    for group in range(3):
        count = min(8, 19 - 8 * group)
        for part in range(4):
            tile = raw[block, 8 * group : 8 * group + count, 1024 * part : 1024 * (part + 1)]
            tile = tile.reshape(count, 8, 128)
            for k in range(count):
                cube[block, 8 * group + k, TOP + 8 * part : TOP + 8 * part + 8, :] = tile[k]


def pack_faces(cube, packets, block, slot):
    row, lane = grid_iotas()
    even = row % 2 == 0
    for face in range(2):
        start = TOP if face == 0 else TOP + 30
        for k in range(5):
            at = 10 * face + 2 * k
            packets[slot, at : at + 2, :] = cube[block, LEAVING[face][k], start : start + 2, :]
    for v in range(4):
        base = TOP + 8 * v
        kept = jnp.zeros((8, 128), jnp.float32)
        for k in range(5):
            far = cube[block, LEAVING[3][k], base + 1 : base + 9, :]
            near = cube[block, LEAVING[2][k], base - 1 : base + 7, :]
            moved = turned(jnp.where(even, far, near), 16 * (k + 1))
            kept = jnp.where(lane // 16 == jnp.where(even, k, k + 1), moved, kept)
        packets[slot, Y_ROW + 8 * v : Y_ROW + 8 * v + 8, :] = kept
        kept = jnp.zeros((8, 128), jnp.float32)
        for k in range(5):
            near = cube[block, LEAVING[4][k], base : base + 8, :]
            far = cube[block, LEAVING[5][k], base : base + 8, :]
            moved = turned(jnp.where(lane % 16 == 15, far, near), 2 * k + 1)
            kept = jnp.where(lane % 16 // 2 == k, moved, kept)
        packets[slot, Z_ROW + 8 * v : Z_ROW + 8 * v + 8, :] = kept


def assemble(packets, nbr, sub, block, first, out, slot, mark):
    row, lane = grid_iotas()
    at, valid = [], []
    for face in range(6):
        near = nbr[block, face]
        valid.append(jnp.full((8, 128), near, jnp.int32) >= 0)
        at.append(jnp.clip(near - first, 0, 11))
    for face in range(2):
        other = 10 * (face ^ 1)
        for start, rows in ((0, 8), (8, 2)):
            value = packets[at[face], other + start : other + start + rows, :]
            out[slot, 10 * face + start : 10 * face + start + rows, :] = jnp.where(
                valid[face][:rows], value, -1.0
            )
    for v in range(4):
        rows = slice(Y_ROW + 8 * v, Y_ROW + 8 * v + 8)
        even_rows = jnp.where(valid[2], packets[at[2], rows, :], -1.0)
        odd_rows = jnp.where(valid[3], packets[at[3], rows, :], -1.0)
        out[slot, rows, :] = jnp.where(row % 2 == 0, even_rows, odd_rows)
        rows = slice(Z_ROW + 8 * v, Z_ROW + 8 * v + 8)
        low = jnp.where(valid[4], packets[at[4], rows, :], -1.0)
        high = jnp.where(valid[5], packets[at[5], rows, :], -1.0)
        out[slot, rows, :] = jnp.where(lane % 2 == 0, low, high)
    count = jnp.full((1, 128), sub[block], jnp.int32).astype(jnp.float32)
    out[slot, COUNT_ROW : COUNT_ROW + 1, :] = count
    out[slot, SLOT_ROW : SLOT_ROW + 1, :] = jnp.full((1, 128), mark, jnp.int32).astype(jnp.float32)


def outside(which, v):
    row, lane = grid_iotas()
    cx, cy, cz = VELOCITY[which]
    x_mask = y_mask = z_mask = None
    if cx == 1 and v == 0:
        x_mask = row < 2
    if cx == -1 and v == 3:
        x_mask = row >= 6
    if cy == 1:
        y_mask = (row % 2 == 0) & (lane < 16)
    if cy == -1:
        y_mask = (row % 2 == 1) & (lane >= 112)
    if cz == 1:
        z_mask = lane % 16 == 0
    if cz == -1:
        z_mask = lane % 16 == 15
    return x_mask, y_mask, z_mask


def build_halo(face_in, slot, halo):
    row, lane = grid_iotas()
    for which in range(1, 19):
        cx, cy, cz = VELOCITY[which]
        for v in range(4):
            x_mask, y_mask, z_mask = outside(which, v)
            value = None
            if z_mask is not None:
                face = 4 if cz == 1 else 5
                k = LEAVING[face ^ 1].index(which)
                by = 16 * cy - (2 * k + 1) + (-15 if cz == 1 else 15)
                start = Z_ROW + 8 * v - 2 * cx
                value = turned(face_in[slot, start : start + 8, :], by)
                if cy != 0:
                    start = start - cy
                    beside = turned(face_in[slot, start : start + 8, :], by)
                    value = jnp.where(lane < 16 if cy == 1 else lane >= 112, beside, value)
            if y_mask is not None:
                face = 2 if cy == 1 else 3
                k = LEAVING[face ^ 1].index(which)
                by = -16 * k if cy == 1 else 112 - 16 * (k + 1)
                start = Y_ROW + 8 * v - 2 * cx
                plane = face_in[slot, start : start + 8, :]
                line = turned(plane, by)
                if cz != 0:
                    line = jnp.where(lane % 16 == (0 if cz == 1 else 15), line, turned(plane, by + cz))
                value = line if value is None else jnp.where(y_mask, line, value)
            if x_mask is not None:
                face = 0 if cx == 1 else 1
                k = LEAVING[face ^ 1].index(which)
                at = 10 * face + 2 * k
                pair = face_in[slot, at : at + 2, :]
                upper, lower = pair[0:1], pair[1:2]
                if cy == 1:
                    high, low = turned(upper, 16), turned(lower, 16)
                    lane1 = lane[0:1]
                    lower = jnp.where(lane1 < 16, high, low)
                    upper = jnp.where(lane1 < 16, upper, high)
                elif cy == -1:
                    high, low = turned(upper, -16), turned(lower, -16)
                    lane1 = lane[0:1]
                    upper = jnp.where(lane1 >= 112, low, high)
                    lower = jnp.where(lane1 >= 112, lower, low)
                elif cz != 0:
                    edge = lane[0:1] % 16 == (0 if cz == 1 else 15)
                    upper = jnp.where(edge, upper, turned(upper, cz))
                    lower = jnp.where(edge, lower, turned(lower, cz))
                spread = jnp.where(
                    row % 2 == 0,
                    jnp.broadcast_to(upper, (8, 128)),
                    jnp.broadcast_to(lower, (8, 128)),
                )
                value = spread if value is None else jnp.where(x_mask, spread, value)
            if value is not None:
                halo[which, 8 * v : 8 * v + 8, :] = value


def collide(f, shear):
    s = {q: f[q] + f[q + 1] for q in range(1, 19, 2)}
    d = {q: f[q] - f[q + 1] for q in range(1, 19, 2)}
    sx, sy, sz = s[1], s[3], s[5]
    sxy, sxz, syz = s[7] + s[9], s[11] + s[13], s[15] + s[17]
    along = sx + (sy + sz)
    across = sxy + (sxz + syz)
    xa, xb = d[7] + d[9], d[11] + d[13]
    ya, yb = d[15] + d[17], d[7] - d[9]
    za, zb = d[11] - d[13], d[15] - d[17]
    x_sum, y_sum, z_sum = xa + xb, ya + yb, za + zb
    jx, jy, jz = d[1] + x_sum, d[3] + y_sum, d[5] + z_sum
    xx, yy, zz = jx * jx, jy * jy, jz * jz
    yz_sum = yy + zz
    jj = xx + yz_sum
    e1 = (1.19 * 19.0 / 2394.0) * ((across - f[0]) - jj)
    e2 = (1.4 / 252.0) * ((9.0 * f[0] - 7.0 * along) - (2.0 * across - 5.5 * jj))
    qx = (1.2 / 40.0 * 5.0 / 3.0) * (x_sum - 2.0 * d[1])
    qy = (1.2 / 40.0 * 5.0 / 3.0) * (y_sum - 2.0 * d[3])
    qz = (1.2 / 40.0 * 5.0 / 3.0) * (z_sum - 2.0 * d[5])
    axial = (2.0 * sx) - (sy + sz)
    planar = (sxy + sxz) - 2.0 * syz
    stress = 2.0 * xx - yz_sum
    e9 = (shear * (1.0 / 36.0)) * ((axial + planar) - stress)
    e10 = (1.4 / 72.0) * ((planar - 2.0 * axial) + 0.5 * stress)
    axial_w = sy - sz
    planar_w = sxy - sxz
    stress_w = yy - zz
    e11 = (shear * (1.0 / 12.0)) * ((axial_w + planar_w) - stress_w)
    e12 = (1.4 / 24.0) * ((planar_w - 2.0 * axial_w) + 0.5 * stress_w)
    quarter = shear * 0.25
    e13 = quarter * ((s[7] - s[9]) - jx * jy)
    e14 = quarter * ((s[15] - s[17]) - jy * jz)
    e15 = quarter * ((s[11] - s[13]) - jx * jz)
    e16 = (1.98 / 8.0) * (xa - xb)
    e17 = (1.98 / 8.0) * (ya - yb)
    e18 = (1.98 / 8.0) * (za - zb)
    post = [None] * 19
    post[0] = f[0] + (30.0 * e1 - 12.0 * e2)
    base = 11.0 * e1 + 4.0 * e2
    t9 = e9 - 2.0 * e10
    t11 = e11 - 2.0 * e12
    evens = {1: 2.0 * t9 - base, 3: t11 - (t9 + base), 5: -((t11 + t9) + base)}
    base = 8.0 * e1 + e2
    u9 = e9 + e10
    u11 = e11 + e12
    upper, lower, third = base + u9 + u11, base + u9 - u11, base - 2.0 * u9
    evens.update({7: upper + e13, 9: upper - e13, 11: lower + e15, 13: lower - e15, 15: third + e14, 17: third - e14})
    xp, xm = qx + e16, qx - e16
    yp, ym = qy + e17, qy - e17
    zp, zm = qz + e18, qz - e18
    odds = {
        1: -4.0 * qx, 3: -4.0 * qy, 5: -4.0 * qz,
        7: xp + ym, 9: xp - ym, 11: xm + zp, 13: xm - zp, 15: yp + zm, 17: yp - zm,
    }
    for q in range(1, 19, 2):
        post[q] = f[q] - (evens[q] + odds[q])
        post[q + 1] = f[q + 1] - (evens[q] - odds[q])
    return post


def cycle(step, state, slot, post, halo, count, shear):
    _, lane = grid_iotas()
    for v in range(4):
        rows = slice(8 * v, 8 * v + 8)
        values = collide([state[slot, q, rows, :] for q in range(19)], shear)
        for q in range(19):
            post[q, TOP + 8 * v : TOP + 8 * v + 8, :] = values[q]
    active = count > step
    for q in range(19):
        cx, cy, cz = VELOCITY[q]
        for v in range(4):
            rows = slice(8 * v, 8 * v + 8)
            start = TOP + 8 * v - 2 * cx
            value = post[q, start : start + 8, :]
            by = 16 * cy + cz
            if cy != 0:
                beside = post[q, start - cy : start - cy + 8, :]
                value = jnp.where(lane >= 128 - by if cy == 1 else lane < -by, beside, value)
            value = turned(value, by)
            masks = [m for m in outside(q, v) if m is not None]
            if masks:
                edge = halo[q, rows, :]
                bounced = post[OPPOSITE[q], TOP + 8 * v : TOP + 8 * v + 8, :]
                value = jnp.where(
                    functools.reduce(jnp.logical_or, masks), jnp.where(edge < 0.0, bounced, edge), value
                )
            state[slot, q, rows, :] = jnp.where(active, value, state[slot, q, rows, :])


def kernel(
    sizes, pop, nbr, sub, moves, out, ids, raw, cube, packets, gone, interface_out, state, interface, post, halo,
    load_sem, send_sem, recv_sem,
):
    ny, nz, total = sizes
    bit = ny * nz
    me = lax.axis_index("gx") * bit + lax.axis_index("gy") * nz + lax.axis_index("gz")

    def place(d):
        return (d // bit, d // nz % ny, d % nz)

    partner_id = lax.rem(me // bit, 2) * (-2 * bit) + bit + me
    partner = place(partner_id)
    later = place(lax.rem(me + 1, total))
    before = place(lax.rem(me + total - 1, total))

    barrier = pltpu.get_barrier_semaphore()
    for other in (partner, before, later):
        pl.semaphore_signal(barrier, inc=1, device_id=other, device_id_type=MESH)

    loads = [pltpu.make_async_copy(pop.at[b], raw.at[b], load_sem.at[b]) for b in range(4)]
    for load in loads:
        load.start()
    for load in loads:
        load.wait()

    def prepare(b, carry):
        unpacked(raw, cube, b)
        pack_faces(cube, packets, b, b + 4)
        return carry

    lax.fori_loop(0, 4, prepare, 0)

    pl.semaphore_wait(barrier, 3)

    def remote(source, target, number, device):
        return pltpu.make_async_remote_copy(
            src_ref=source,
            dst_ref=target,
            send_sem=send_sem.at[number],
            recv_sem=recv_sem.at[number],
            device_id=device,
            device_id_type=MESH,
        )

    mine = packets.at[pl.ds(4, 4), pl.ds(0, SENT_ROWS)]
    to_later = remote(mine, packets.at[pl.ds(0, 4), pl.ds(0, SENT_ROWS)], 0, later)
    to_before = remote(mine, packets.at[pl.ds(8, 4), pl.ds(0, SENT_ROWS)], 1, before)
    to_later.start()
    to_before.start()

    moved = [moves[0, 0], moves[0, 1]]
    blocks = []
    for k in range(2):
        def take(q, carry, k=k):
            gone[k, q] = cube[moved[k], q, TOP : TOP + 32, :]
            return carry

        lax.fori_loop(0, 19, take, 0)
        copy = remote(gone.at[k], state.at[2 + k], 2 + k, partner)
        copy.start()
        blocks.append(copy)

    to_later.wait_recv()
    to_before.wait_recv()

    first = (me - 1) * 4
    faces = []
    for k in range(2):
        assemble(packets, nbr, sub, moved[k], first, interface_out, k, moved[k])
        copy = remote(interface_out.at[k], interface.at[2 + k], 4 + k, partner)
        copy.start()
        faces.append(copy)

    low = jnp.minimum(moved[0], moved[1])
    high = jnp.maximum(moved[0], moved[1])
    stay0 = jnp.where(low > 0, 0, jnp.where(high > 1, 1, 2))
    stay1 = jnp.minimum(6 - low - high - stay0, 3)

    for j, stay in enumerate((stay0, stay1)):
        assemble(packets, nbr, sub, stay, first, interface, j, stay)

        def keep(q, carry, j=j, stay=stay):
            state[j, q] = cube[stay, q, TOP : TOP + 32, :]
            return carry

        lax.fori_loop(0, 19, keep, 0)

    def job(j, carry):
        for k in range(2):
            @pl.when(j == 2 + k)
            def _(k=k):
                faces[k].wait_recv()
                blocks[k].wait_recv()

        count = jnp.broadcast_to(interface[j, COUNT_ROW : COUNT_ROW + 1, :], (8, 128))
        shear = 1.0 / (count * (1.0 / 1.6 - 0.5) + 0.5)
        build_halo(interface, j, halo)

        def one(step, carry):
            at = jnp.full((8, 128), step, jnp.int32).astype(jnp.float32)
            cycle(at, state, j, post, halo, count, shear)
            return carry

        return lax.fori_loop(0, 4, one, carry)

    lax.fori_loop(0, 4, job, 0)

    for s in range(4):
        source = jnp.where(
            moved[0] == s, 2, jnp.where(moved[1] == s, 3, jnp.where(stay0 == s, 0, 1))
        )
        for group in range(3):
            count = min(8, 19 - 8 * group)
            for part in range(4):
                tile = state[source, 8 * group : 8 * group + count, 8 * part : 8 * part + 8, :]
                out[s, 8 * group : 8 * group + count, 1024 * part : 1024 * (part + 1)] = tile.reshape(count, 1024)

    marks = [
        jnp.max(interface[2 + k, SLOT_ROW : SLOT_ROW + 1, :]).astype(jnp.int32) + partner_id * 4 for k in range(2)
    ]
    for s in range(4):
        ids[s] = jnp.where(moved[0] == s, marks[0], jnp.where(moved[1] == s, marks[1], me * 4 + s))

    to_later.wait_send()
    to_before.wait_send()
    for k in range(2):
        blocks[k].wait_send()
        faces[k].wait_send()


def shards(sizes, populations, neighbours, substeps, moves):
    f32 = jnp.float32
    return pl.pallas_call(
        functools.partial(kernel, sizes),
        out_shape=(jax.ShapeDtypeStruct((4, 19, 4096), f32), jax.ShapeDtypeStruct((4,), jnp.int32)),
        in_specs=[
            pl.BlockSpec(memory_space=pl.ANY),
            pl.BlockSpec(memory_space=pltpu.SMEM),
            pl.BlockSpec(memory_space=pltpu.SMEM),
            pl.BlockSpec(memory_space=pltpu.SMEM),
        ],
        out_specs=(pl.BlockSpec(memory_space=pltpu.VMEM), pl.BlockSpec(memory_space=pltpu.SMEM)),
        scratch_shapes=[
            pltpu.VMEM((4, 19, 4096), f32),
            pltpu.VMEM((4, 19, 48, 128), f32),
            pltpu.VMEM((12, PACKET_ROWS, 128), f32),
            pltpu.VMEM((2, 19, 32, 128), f32),
            pltpu.VMEM((2, PACKET_ROWS, 128), f32),
            pltpu.VMEM((4, 19, 32, 128), f32),
            pltpu.VMEM((4, PACKET_ROWS, 128), f32),
            pltpu.VMEM((19, 48, 128), f32),
            pltpu.VMEM((19, 32, 128), f32),
            pltpu.SemaphoreType.DMA((4,)),
            pltpu.SemaphoreType.DMA((6,)),
            pltpu.SemaphoreType.DMA((6,)),
        ],
        compiler_params=pltpu.CompilerParams(
            collective_id=0, has_side_effects=True, vmem_limit_bytes=40 * 1024 * 1024
        ),
        name="lattice_step",
    )(populations, neighbours, substeps, moves)


def solution(mesh):
    sizes = (mesh.shape["gy"], mesh.shape["gz"], mesh.size)
    return jax.shard_map(
        functools.partial(shards, sizes),
        mesh=mesh,
        in_specs=(P(AXES, None, None), P(AXES, None), P(AXES), P(AXES, None)),
        out_specs=(P(AXES, None, None), P(AXES)),
        check_vma=False,
    )
```

```python
import functools

import jax
import jax.numpy as jnp
import numpy as np
from jax import lax
from jax.experimental import pallas as pl
from jax.experimental.pallas import tpu as pltpu
from jax.sharding import PartitionSpec as P

MESH = pl.DeviceIdType.MESH
AXES = ("gx", "gy", "gz")
VELOCITY = [
    (0, 0, 0), (1, 0, 0), (-1, 0, 0), (0, 1, 0), (0, -1, 0), (0, 0, 1), (0, 0, -1),
    (1, 1, 0), (-1, -1, 0), (1, -1, 0), (-1, 1, 0), (1, 0, 1), (-1, 0, -1),
    (1, 0, -1), (-1, 0, 1), (0, 1, 1), (0, -1, -1), (0, 1, -1), (0, -1, 1),
]
OPPOSITE = [0, 2, 1, 4, 3, 6, 5, 8, 7, 10, 9, 12, 11, 14, 13, 16, 15, 18, 17]
LEAVING = [
    [2, 8, 10, 12, 14], [1, 7, 9, 11, 13], [4, 8, 9, 16, 18],
    [3, 7, 10, 15, 17], [6, 12, 13, 16, 17], [5, 11, 14, 15, 18],
]
COUNT_ROW, SLOT_ROW, Y_ROW, Z_ROW, SENT_ROWS, PACKET_ROWS = 20, 21, 24, 56, 88, 96
TOP = 8


def turned(value, by):
    by = by % 128
    return value if by == 0 else pltpu.roll(value, by, 1)


def grid_iotas():
    row = lax.broadcasted_iota(jnp.int32, (8, 128), 0)
    lane = lax.broadcasted_iota(jnp.int32, (8, 128), 1)
    return row, lane


def unpacked(raw, cube, block):
    for q in range(19):
        for v in range(4):
            cube[block, q, TOP + 8 * v : TOP + 8 * v + 8, :] = raw[q, pl.ds(32 * v + block, 8, stride=4), :]


def pack_faces(cube, packets, block, slot):
    row, lane = grid_iotas()
    even = row % 2 == 0
    for face in range(2):
        start = TOP if face == 0 else TOP + 30
        for k in range(5):
            at = 10 * face + 2 * k
            packets[slot, at : at + 2, :] = cube[block, LEAVING[face][k], start : start + 2, :]
    for v in range(4):
        base = TOP + 8 * v
        kept = jnp.zeros((8, 128), jnp.float32)
        for k in range(5):
            far = cube[block, LEAVING[3][k], base + 1 : base + 9, :]
            near = cube[block, LEAVING[2][k], base - 1 : base + 7, :]
            moved = turned(jnp.where(even, far, near), 16 * (k + 1))
            kept = jnp.where(lane // 16 == jnp.where(even, k, k + 1), moved, kept)
        packets[slot, Y_ROW + 8 * v : Y_ROW + 8 * v + 8, :] = kept
        kept = jnp.zeros((8, 128), jnp.float32)
        for k in range(5):
            near = cube[block, LEAVING[4][k], base : base + 8, :]
            far = cube[block, LEAVING[5][k], base : base + 8, :]
            moved = turned(jnp.where(lane % 16 == 15, far, near), 2 * k + 1)
            kept = jnp.where(lane % 16 // 2 == k, moved, kept)
        packets[slot, Z_ROW + 8 * v : Z_ROW + 8 * v + 8, :] = kept


def assemble(packets, nbr, sub, block, first, out, slot, mark):
    row, lane = grid_iotas()
    at, valid = [], []
    for face in range(6):
        near = nbr[block, face]
        valid.append(jnp.full((8, 128), near, jnp.int32) >= 0)
        at.append(jnp.clip(near - first, 0, 11))
    for face in range(2):
        other = 10 * (face ^ 1)
        for start, rows in ((0, 8), (8, 2)):
            value = packets[at[face], other + start : other + start + rows, :]
            out[slot, 10 * face + start : 10 * face + start + rows, :] = jnp.where(
                valid[face][:rows], value, -1.0
            )
    for v in range(4):
        rows = slice(Y_ROW + 8 * v, Y_ROW + 8 * v + 8)
        even_rows = jnp.where(valid[2], packets[at[2], rows, :], -1.0)
        odd_rows = jnp.where(valid[3], packets[at[3], rows, :], -1.0)
        out[slot, rows, :] = jnp.where(row % 2 == 0, even_rows, odd_rows)
        rows = slice(Z_ROW + 8 * v, Z_ROW + 8 * v + 8)
        low = jnp.where(valid[4], packets[at[4], rows, :], -1.0)
        high = jnp.where(valid[5], packets[at[5], rows, :], -1.0)
        out[slot, rows, :] = jnp.where(lane % 2 == 0, low, high)
    count = jnp.full((1, 128), sub[block], jnp.int32).astype(jnp.float32)
    out[slot, COUNT_ROW : COUNT_ROW + 1, :] = count
    out[slot, SLOT_ROW : SLOT_ROW + 1, :] = jnp.full((1, 128), mark, jnp.int32).astype(jnp.float32)


def outside(which, v):
    row, lane = grid_iotas()
    cx, cy, cz = VELOCITY[which]
    x_mask = y_mask = z_mask = None
    if cx == 1 and v == 0:
        x_mask = row < 2
    if cx == -1 and v == 3:
        x_mask = row >= 6
    if cy == 1:
        y_mask = (row % 2 == 0) & (lane < 16)
    if cy == -1:
        y_mask = (row % 2 == 1) & (lane >= 112)
    if cz == 1:
        z_mask = lane % 16 == 0
    if cz == -1:
        z_mask = lane % 16 == 15
    return x_mask, y_mask, z_mask


def build_halo(face_in, slot, halo):
    row, lane = grid_iotas()
    for which in range(1, 19):
        cx, cy, cz = VELOCITY[which]
        for v in range(4):
            x_mask, y_mask, z_mask = outside(which, v)
            value = None
            if z_mask is not None:
                face = 4 if cz == 1 else 5
                k = LEAVING[face ^ 1].index(which)
                by = 16 * cy - (2 * k + 1) + (-15 if cz == 1 else 15)
                start = Z_ROW + 8 * v - 2 * cx
                value = turned(face_in[slot, start : start + 8, :], by)
                if cy != 0:
                    start = start - cy
                    beside = turned(face_in[slot, start : start + 8, :], by)
                    value = jnp.where(lane < 16 if cy == 1 else lane >= 112, beside, value)
            if y_mask is not None:
                face = 2 if cy == 1 else 3
                k = LEAVING[face ^ 1].index(which)
                by = -16 * k if cy == 1 else 112 - 16 * (k + 1)
                start = Y_ROW + 8 * v - 2 * cx
                plane = face_in[slot, start : start + 8, :]
                line = turned(plane, by)
                if cz != 0:
                    line = jnp.where(lane % 16 == (0 if cz == 1 else 15), line, turned(plane, by + cz))
                value = line if value is None else jnp.where(y_mask, line, value)
            if x_mask is not None:
                face = 0 if cx == 1 else 1
                k = LEAVING[face ^ 1].index(which)
                at = 10 * face + 2 * k
                pair = face_in[slot, at : at + 2, :]
                upper, lower = pair[0:1], pair[1:2]
                if cy == 1:
                    high, low = turned(upper, 16), turned(lower, 16)
                    lane1 = lane[0:1]
                    lower = jnp.where(lane1 < 16, high, low)
                    upper = jnp.where(lane1 < 16, upper, high)
                elif cy == -1:
                    high, low = turned(upper, -16), turned(lower, -16)
                    lane1 = lane[0:1]
                    upper = jnp.where(lane1 >= 112, low, high)
                    lower = jnp.where(lane1 >= 112, lower, low)
                elif cz != 0:
                    edge = lane[0:1] % 16 == (0 if cz == 1 else 15)
                    upper = jnp.where(edge, upper, turned(upper, cz))
                    lower = jnp.where(edge, lower, turned(lower, cz))
                spread = jnp.where(
                    row % 2 == 0,
                    jnp.broadcast_to(upper, (8, 128)),
                    jnp.broadcast_to(lower, (8, 128)),
                )
                value = spread if value is None else jnp.where(x_mask, spread, value)
            if value is not None:
                halo[which, 8 * v : 8 * v + 8, :] = value


def collide(f, shear):
    s = {q: f[q] + f[q + 1] for q in range(1, 19, 2)}
    d = {q: f[q] - f[q + 1] for q in range(1, 19, 2)}
    sx, sy, sz = s[1], s[3], s[5]
    sxy, sxz, syz = s[7] + s[9], s[11] + s[13], s[15] + s[17]
    along = sx + (sy + sz)
    across = sxy + (sxz + syz)
    xa, xb = d[7] + d[9], d[11] + d[13]
    ya, yb = d[15] + d[17], d[7] - d[9]
    za, zb = d[11] - d[13], d[15] - d[17]
    x_sum, y_sum, z_sum = xa + xb, ya + yb, za + zb
    jx, jy, jz = d[1] + x_sum, d[3] + y_sum, d[5] + z_sum
    xx, yy, zz = jx * jx, jy * jy, jz * jz
    yz_sum = yy + zz
    jj = xx + yz_sum
    e1 = (1.19 * 19.0 / 2394.0) * ((across - f[0]) - jj)
    e2 = (1.4 / 252.0) * ((9.0 * f[0] - 7.0 * along) - (2.0 * across - 5.5 * jj))
    qx = (1.2 / 40.0 * 5.0 / 3.0) * (x_sum - 2.0 * d[1])
    qy = (1.2 / 40.0 * 5.0 / 3.0) * (y_sum - 2.0 * d[3])
    qz = (1.2 / 40.0 * 5.0 / 3.0) * (z_sum - 2.0 * d[5])
    axial = (2.0 * sx) - (sy + sz)
    planar = (sxy + sxz) - 2.0 * syz
    stress = 2.0 * xx - yz_sum
    e9 = (shear * (1.0 / 36.0)) * ((axial + planar) - stress)
    e10 = (1.4 / 72.0) * ((planar - 2.0 * axial) + 0.5 * stress)
    axial_w = sy - sz
    planar_w = sxy - sxz
    stress_w = yy - zz
    e11 = (shear * (1.0 / 12.0)) * ((axial_w + planar_w) - stress_w)
    e12 = (1.4 / 24.0) * ((planar_w - 2.0 * axial_w) + 0.5 * stress_w)
    quarter = shear * 0.25
    e13 = quarter * ((s[7] - s[9]) - jx * jy)
    e14 = quarter * ((s[15] - s[17]) - jy * jz)
    e15 = quarter * ((s[11] - s[13]) - jx * jz)
    e16 = (1.98 / 8.0) * (xa - xb)
    e17 = (1.98 / 8.0) * (ya - yb)
    e18 = (1.98 / 8.0) * (za - zb)
    post = [None] * 19
    post[0] = f[0] + (30.0 * e1 - 12.0 * e2)
    base = 11.0 * e1 + 4.0 * e2
    t9 = e9 - 2.0 * e10
    t11 = e11 - 2.0 * e12
    evens = {1: 2.0 * t9 - base, 3: t11 - (t9 + base), 5: -((t11 + t9) + base)}
    base = 8.0 * e1 + e2
    u9 = e9 + e10
    u11 = e11 + e12
    upper, lower, third = base + u9 + u11, base + u9 - u11, base - 2.0 * u9
    evens.update({7: upper + e13, 9: upper - e13, 11: lower + e15, 13: lower - e15, 15: third + e14, 17: third - e14})
    xp, xm = qx + e16, qx - e16
    yp, ym = qy + e17, qy - e17
    zp, zm = qz + e18, qz - e18
    odds = {
        1: -4.0 * qx, 3: -4.0 * qy, 5: -4.0 * qz,
        7: xp + ym, 9: xp - ym, 11: xm + zp, 13: xm - zp, 15: yp + zm, 17: yp - zm,
    }
    for q in range(1, 19, 2):
        post[q] = f[q] - (evens[q] + odds[q])
        post[q + 1] = f[q + 1] - (evens[q] - odds[q])
    return post


def cycle(step, state, slot, post, halo, count, shear):
    _, lane = grid_iotas()
    for v in range(4):
        rows = slice(8 * v, 8 * v + 8)
        values = collide([state[slot, q, rows, :] for q in range(19)], shear)
        for q in range(19):
            post[q, TOP + 8 * v : TOP + 8 * v + 8, :] = values[q]
    active = count > step
    for q in range(19):
        cx, cy, cz = VELOCITY[q]
        for v in range(4):
            rows = slice(8 * v, 8 * v + 8)
            start = TOP + 8 * v - 2 * cx
            value = post[q, start : start + 8, :]
            by = 16 * cy + cz
            if cy != 0:
                beside = post[q, start - cy : start - cy + 8, :]
                value = jnp.where(lane >= 128 - by if cy == 1 else lane < -by, beside, value)
            value = turned(value, by)
            masks = [m for m in outside(q, v) if m is not None]
            if masks:
                edge = halo[q, rows, :]
                bounced = post[OPPOSITE[q], TOP + 8 * v : TOP + 8 * v + 8, :]
                value = jnp.where(
                    functools.reduce(jnp.logical_or, masks), jnp.where(edge < 0.0, bounced, edge), value
                )
            state[slot, q, rows, :] = jnp.where(active, value, state[slot, q, rows, :])


def kernel(
    sizes, pop, nbr, sub, moves, out, ids, raw, cube, packets, gone, interface_out, state, interface, post, halo,
    load_sem, send_sem, recv_sem, answer_sem, near_sem, across_sem,
):
    ny, nz, total = sizes
    bit = ny * nz
    me = lax.axis_index("gx") * bit + lax.axis_index("gy") * nz + lax.axis_index("gz")

    def place(d):
        return (d // bit, d // nz % ny, d % nz)

    partner_id = lax.rem(me // bit, 2) * (-2 * bit) + bit + me
    partner = place(partner_id)
    later = place(lax.rem(me + 1, total))
    before = place(lax.rem(me + total - 1, total))

    odd = lax.rem(me // bit, 2) == 1
    inner = lax.rem(me, bit)
    at_start, at_end = inner == 0, inner == bit - 1
    even = jnp.logical_not(odd)
    barrier = pltpu.get_barrier_semaphore()

    def signal(semaphore, device):
        pl.semaphore_signal(semaphore, inc=1, device_id=device, device_id_type=MESH)

    @pl.when(odd)
    def _():
        signal(barrier, partner)

    @pl.when(even & at_start)
    def _():
        signal(barrier, before)

    @pl.when(even & at_end)
    def _():
        signal(barrier, later)

    load = pltpu.make_async_copy(pop, raw, load_sem)
    load.start()
    load.wait()

    for b in range(4):
        unpacked(raw, cube, b)

    def prepare(b, carry):
        pack_faces(cube, packets, b, b + 4)
        return carry

    lax.fori_loop(0, 4, prepare, 0)

    @pl.when(even)
    def _():
        pl.semaphore_wait(barrier, 1)
        signal(answer_sem, partner)

    @pl.when(odd)
    def _():
        pl.semaphore_wait(answer_sem, 1)

    @pl.when(odd & jnp.logical_not(at_start))
    def _():
        signal(barrier, before)

    @pl.when(odd & jnp.logical_not(at_end))
    def _():
        signal(barrier, later)

    def remote(source, target, number, device):
        return pltpu.make_async_remote_copy(
            src_ref=source,
            dst_ref=target,
            send_sem=send_sem.at[number],
            recv_sem=recv_sem.at[number],
            device_id=device,
            device_id_type=MESH,
        )

    moved = [moves[0, 0], moves[0, 1]]
    blocks = []
    for k in range(2):
        def take(q, carry, k=k):
            gone[k, q] = cube[moved[k], q, TOP : TOP + 32, :]
            return carry

        lax.fori_loop(0, 19, take, 0)
        copy = remote(gone.at[k], state.at[2 + k], 2 + k, partner)
        copy.start()
        blocks.append(copy)

    @pl.when(odd)
    def _():
        pl.semaphore_wait(barrier, 2)
        signal(near_sem, partner)

    @pl.when(odd & at_start)
    def _():
        signal(across_sem, before)

    @pl.when(odd & at_end)
    def _():
        signal(across_sem, later)

    @pl.when(even)
    def _():
        pl.semaphore_wait(near_sem, 1)

    @pl.when(even & (at_start | at_end))
    def _():
        pl.semaphore_wait(across_sem, 1)

    mine = packets.at[pl.ds(4, 4), pl.ds(0, SENT_ROWS)]
    to_later = remote(mine, packets.at[pl.ds(0, 4), pl.ds(0, SENT_ROWS)], 0, later)
    to_before = remote(mine, packets.at[pl.ds(8, 4), pl.ds(0, SENT_ROWS)], 1, before)
    to_later.start()
    to_before.start()

    to_later.wait_recv()
    to_before.wait_recv()

    first = (me - 1) * 4
    faces = []
    for k in range(2):
        assemble(packets, nbr, sub, moved[k], first, interface_out, k, moved[k])
        copy = remote(interface_out.at[k], interface.at[2 + k], 4 + k, partner)
        copy.start()
        faces.append(copy)

    low = jnp.minimum(moved[0], moved[1])
    high = jnp.maximum(moved[0], moved[1])
    stay0 = jnp.where(low > 0, 0, jnp.where(high > 1, 1, 2))
    stay1 = jnp.minimum(6 - low - high - stay0, 3)

    for j, stay in enumerate((stay0, stay1)):
        assemble(packets, nbr, sub, stay, first, interface, j, stay)

        def keep(q, carry, j=j, stay=stay):
            state[j, q] = cube[stay, q, TOP : TOP + 32, :]
            return carry

        lax.fori_loop(0, 19, keep, 0)

    def job(j, carry):
        for k in range(2):
            @pl.when(j == 2 + k)
            def _(k=k):
                faces[k].wait_recv()
                blocks[k].wait_recv()

        count = jnp.broadcast_to(interface[j, COUNT_ROW : COUNT_ROW + 1, :], (8, 128))
        shear = 1.0 / (count * (1.0 / 1.6 - 0.5) + 0.5)
        build_halo(interface, j, halo)

        def one(step, carry):
            at = jnp.full((8, 128), step, jnp.int32).astype(jnp.float32)
            cycle(at, state, j, post, halo, count, shear)
            return carry

        return lax.fori_loop(0, 4, one, carry)

    lax.fori_loop(0, 4, job, 0)

    for s in range(4):
        source = jnp.where(
            moved[0] == s, 2, jnp.where(moved[1] == s, 3, jnp.where(stay0 == s, 0, 1))
        )
        for q in range(19):
            for v in range(4):
                out[q, pl.ds(32 * v + s, 8, stride=4), :] = state[source, q, 8 * v : 8 * v + 8, :]

    marks = [
        jnp.max(interface[2 + k, SLOT_ROW : SLOT_ROW + 1, :]).astype(jnp.int32) + partner_id * 4 for k in range(2)
    ]
    for s in range(4):
        ids[s] = jnp.where(moved[0] == s, marks[0], jnp.where(moved[1] == s, marks[1], me * 4 + s))

    to_later.wait_send()
    to_before.wait_send()
    for k in range(2):
        blocks[k].wait_send()
        faces[k].wait_send()


def shards(sizes, populations, neighbours, substeps, moves):
    f32 = jnp.float32
    lying = populations.reshape(4, 19, 32, 128).transpose(1, 2, 0, 3).reshape(19, 128, 128)
    result, ids = pl.pallas_call(
        functools.partial(kernel, sizes),
        out_shape=(jax.ShapeDtypeStruct((19, 128, 128), f32), jax.ShapeDtypeStruct((4,), jnp.int32)),
        in_specs=[
            pl.BlockSpec(memory_space=pl.ANY),
            pl.BlockSpec(memory_space=pltpu.SMEM),
            pl.BlockSpec(memory_space=pltpu.SMEM),
            pl.BlockSpec(memory_space=pltpu.SMEM),
        ],
        out_specs=(pl.BlockSpec(memory_space=pltpu.VMEM), pl.BlockSpec(memory_space=pltpu.SMEM)),
        scratch_shapes=[
            pltpu.VMEM((19, 128, 128), f32),
            pltpu.VMEM((4, 19, 48, 128), f32),
            pltpu.VMEM((12, PACKET_ROWS, 128), f32),
            pltpu.VMEM((2, 19, 32, 128), f32),
            pltpu.VMEM((2, PACKET_ROWS, 128), f32),
            pltpu.VMEM((4, 19, 32, 128), f32),
            pltpu.VMEM((4, PACKET_ROWS, 128), f32),
            pltpu.VMEM((19, 48, 128), f32),
            pltpu.VMEM((19, 32, 128), f32),
            pltpu.SemaphoreType.DMA,
            pltpu.SemaphoreType.DMA((6,)),
            pltpu.SemaphoreType.DMA((6,)),
            pltpu.SemaphoreType.REGULAR,
            pltpu.SemaphoreType.REGULAR,
            pltpu.SemaphoreType.REGULAR,
        ],
        compiler_params=pltpu.CompilerParams(
            collective_id=0, has_side_effects=True, vmem_limit_bytes=40 * 1024 * 1024
        ),
        name="lattice_step",
    )(lying, neighbours, substeps, moves)
    return result.reshape(19, 32, 4, 128).transpose(2, 0, 1, 3).reshape(4, 19, 4096), ids


def solution(mesh):
    sizes = (mesh.shape["gy"], mesh.shape["gz"], mesh.size)
    return jax.shard_map(
        functools.partial(shards, sizes),
        mesh=mesh,
        in_specs=(P(AXES, None, None), P(AXES, None), P(AXES), P(AXES, None)),
        out_specs=(P(AXES, None, None), P(AXES)),
        check_vma=False,
    )
```

```python
import functools

import jax
import jax.numpy as jnp
import numpy as np
from jax import lax
from jax.experimental import pallas as pl
from jax.experimental.pallas import tpu as pltpu
from jax.sharding import PartitionSpec as P

MESH = pl.DeviceIdType.MESH
AXES = ("gx", "gy", "gz")
VELOCITY = [
    (0, 0, 0), (1, 0, 0), (-1, 0, 0), (0, 1, 0), (0, -1, 0), (0, 0, 1), (0, 0, -1),
    (1, 1, 0), (-1, -1, 0), (1, -1, 0), (-1, 1, 0), (1, 0, 1), (-1, 0, -1),
    (1, 0, -1), (-1, 0, 1), (0, 1, 1), (0, -1, -1), (0, 1, -1), (0, -1, 1),
]
OPPOSITE = [0, 2, 1, 4, 3, 6, 5, 8, 7, 10, 9, 12, 11, 14, 13, 16, 15, 18, 17]
LEAVING = [
    [2, 8, 10, 12, 14], [1, 7, 9, 11, 13], [4, 8, 9, 16, 18],
    [3, 7, 10, 15, 17], [6, 12, 13, 16, 17], [5, 11, 14, 15, 18],
]
Y_SENT, Z_SENT, X_SENT, COUNT_ROW, SLOT_ROW, SENT_ROWS = 0, 24, 48, 68, 69, 72
X_ROW, Y_ROW, Z_ROW, PLANE_ROWS = 0, 24, 56, 96
TOP = 8


def turned(value, by):
    by = by % 128
    return value if by == 0 else pltpu.roll(value, by, 1)


def grid_iotas():
    row = lax.broadcasted_iota(jnp.int32, (8, 128), 0)
    lane = lax.broadcasted_iota(jnp.int32, (8, 128), 1)
    return row, lane


def unpacked(raw, cube, block):
    for q in range(19):
        for v in range(4):
            cube[block, q, TOP + 8 * v : TOP + 8 * v + 8, :] = raw[q, pl.ds(32 * v + block, 8, stride=4), :]


def pack_faces(cube, packets, block, slot):
    row, lane = grid_iotas()
    even = row % 2 == 0
    place = (lane // 16 - row % 2) % 8
    for face in range(2):
        start = TOP if face == 0 else TOP + 30
        for k in range(5):
            at = X_SENT + 10 * face + 2 * k
            packets[slot, at : at + 2, :] = cube[block, LEAVING[face][k], start : start + 2, :]
    ys, zs = [], []
    for v in range(4):
        base = TOP + 8 * v
        kept = jnp.zeros((8, 128), jnp.float32)
        for k in range(5):
            far = cube[block, LEAVING[3][k], base + 1 : base + 9, :]
            near = cube[block, LEAVING[2][k], base - 1 : base + 7, :]
            moved = turned(jnp.where(even, far, near), 16 * (k + 1))
            kept = jnp.where(place == k, moved, kept)
        ys.append(kept)
        kept = jnp.zeros((8, 128), jnp.float32)
        for k in range(5):
            near = cube[block, LEAVING[4][k], base : base + 8, :]
            far = cube[block, LEAVING[5][k], base : base + 8, :]
            moved = turned(jnp.where(lane % 16 == 15, far, near), 2 * k + 1)
            kept = jnp.where(lane % 16 // 2 == k, moved, kept)
        zs.append(kept)
    ys[0] = jnp.where(place >= 5, turned(ys[3], 80), ys[0])
    ys[1] = jnp.where(place >= 5, turned(ys[3], 32), ys[1])
    zs[0] = jnp.where(lane % 16 >= 10, turned(zs[3], 10), zs[0])
    zs[1] = jnp.where(lane % 16 >= 10, turned(zs[3], 4), zs[1])
    for v in range(3):
        packets[slot, Y_SENT + 8 * v : Y_SENT + 8 * v + 8, :] = ys[v]
        packets[slot, Z_SENT + 8 * v : Z_SENT + 8 * v + 8, :] = zs[v]


def spread(sent, slot, planes):
    row, lane = grid_iotas()
    place = (lane // 16 - row % 2) % 8
    ys = [sent[slot, Y_SENT + 8 * v : Y_SENT + 8 * v + 8, :] for v in range(3)]
    zs = [sent[slot, Z_SENT + 8 * v : Z_SENT + 8 * v + 8, :] for v in range(3)]
    ys.append(jnp.where(place < 3, turned(ys[0], -80), turned(ys[1], -32)))
    zs.append(jnp.where(lane % 16 < 6, turned(zs[0], -10), turned(zs[1], -4)))
    for v in range(4):
        planes[Y_ROW + 8 * v : Y_ROW + 8 * v + 8, :] = ys[v]
        planes[Z_ROW + 8 * v : Z_ROW + 8 * v + 8, :] = zs[v]
    for v in range(3):
        planes[X_ROW + 8 * v : X_ROW + 8 * v + 8, :] = sent[slot, X_SENT + 8 * v : X_SENT + 8 * v + 8, :]


def assemble(packets, plan, block, first, out, slot, mark):
    row, lane = grid_iotas()
    at, valid = [], []
    for face in range(6):
        near = plan[block, face]
        valid.append(jnp.full((8, 128), near, jnp.int32) >= 0)
        at.append(jnp.clip(near - first, 0, 11))
    for face in range(2):
        other = 10 * (face ^ 1)
        for start, rows in ((0, 8), (8, 2)):
            value = packets[at[face], X_SENT + other + start : X_SENT + other + start + rows, :]
            out[slot, X_SENT + 10 * face + start : X_SENT + 10 * face + start + rows, :] = jnp.where(
                valid[face][:rows], value, -1.0
            )
    for v in range(3):
        rows = slice(Y_SENT + 8 * v, Y_SENT + 8 * v + 8)
        even_rows = jnp.where(valid[2], packets[at[2], rows, :], -1.0)
        odd_rows = jnp.where(valid[3], packets[at[3], rows, :], -1.0)
        out[slot, rows, :] = jnp.where(row % 2 == 0, even_rows, odd_rows)
        rows = slice(Z_SENT + 8 * v, Z_SENT + 8 * v + 8)
        low = jnp.where(valid[4], packets[at[4], rows, :], -1.0)
        high = jnp.where(valid[5], packets[at[5], rows, :], -1.0)
        out[slot, rows, :] = jnp.where(lane % 2 == 0, low, high)
    count = jnp.full((1, 128), plan[4, block], jnp.int32).astype(jnp.float32)
    out[slot, COUNT_ROW : COUNT_ROW + 1, :] = count
    out[slot, SLOT_ROW : SLOT_ROW + 1, :] = jnp.full((1, 128), mark, jnp.int32).astype(jnp.float32)


def outside(which, v):
    row, lane = grid_iotas()
    cx, cy, cz = VELOCITY[which]
    x_mask = y_mask = z_mask = None
    if cx == 1 and v == 0:
        x_mask = row < 2
    if cx == -1 and v == 3:
        x_mask = row >= 6
    if cy == 1:
        y_mask = (row % 2 == 0) & (lane < 16)
    if cy == -1:
        y_mask = (row % 2 == 1) & (lane >= 112)
    if cz == 1:
        z_mask = lane % 16 == 0
    if cz == -1:
        z_mask = lane % 16 == 15
    return x_mask, y_mask, z_mask


def build_halo(planes, halo):
    row, lane = grid_iotas()
    for which in range(1, 19):
        cx, cy, cz = VELOCITY[which]
        for v in range(4):
            x_mask, y_mask, z_mask = outside(which, v)
            value = None
            if z_mask is not None:
                face = 4 if cz == 1 else 5
                k = LEAVING[face ^ 1].index(which)
                by = 16 * cy - (2 * k + 1) + (-15 if cz == 1 else 15)
                start = Z_ROW + 8 * v - 2 * cx
                value = turned(planes[start : start + 8, :], by)
                if cy != 0:
                    start = start - cy
                    beside = turned(planes[start : start + 8, :], by)
                    value = jnp.where(lane < 16 if cy == 1 else lane >= 112, beside, value)
            if y_mask is not None:
                face = 2 if cy == 1 else 3
                k = LEAVING[face ^ 1].index(which)
                by = -16 * k if cy == 1 else 112 - 16 * (k + 1)
                start = Y_ROW + 8 * v - 2 * cx
                plane = planes[start : start + 8, :]
                line = turned(plane, by)
                if cz != 0:
                    line = jnp.where(lane % 16 == (0 if cz == 1 else 15), line, turned(plane, by + cz))
                value = line if value is None else jnp.where(y_mask, line, value)
            if x_mask is not None:
                face = 0 if cx == 1 else 1
                k = LEAVING[face ^ 1].index(which)
                at = X_ROW + 10 * face + 2 * k
                pair = planes[at : at + 2, :]
                upper, lower = pair[0:1], pair[1:2]
                if cy == 1:
                    high, low = turned(upper, 16), turned(lower, 16)
                    lane1 = lane[0:1]
                    lower = jnp.where(lane1 < 16, high, low)
                    upper = jnp.where(lane1 < 16, upper, high)
                elif cy == -1:
                    high, low = turned(upper, -16), turned(lower, -16)
                    lane1 = lane[0:1]
                    upper = jnp.where(lane1 >= 112, low, high)
                    lower = jnp.where(lane1 >= 112, lower, low)
                elif cz != 0:
                    edge = lane[0:1] % 16 == (0 if cz == 1 else 15)
                    upper = jnp.where(edge, upper, turned(upper, cz))
                    lower = jnp.where(edge, lower, turned(lower, cz))
                both = jnp.where(
                    row % 2 == 0,
                    jnp.broadcast_to(upper, (8, 128)),
                    jnp.broadcast_to(lower, (8, 128)),
                )
                value = both if value is None else jnp.where(x_mask, both, value)
            if value is not None:
                halo[which, 8 * v : 8 * v + 8, :] = value


def collide(f, shear):
    s = {q: f[q] + f[q + 1] for q in range(1, 19, 2)}
    d = {q: f[q] - f[q + 1] for q in range(1, 19, 2)}
    sx, sy, sz = s[1], s[3], s[5]
    sxy, sxz, syz = s[7] + s[9], s[11] + s[13], s[15] + s[17]
    along = sx + (sy + sz)
    across = sxy + (sxz + syz)
    xa, xb = d[7] + d[9], d[11] + d[13]
    ya, yb = d[15] + d[17], d[7] - d[9]
    za, zb = d[11] - d[13], d[15] - d[17]
    x_sum, y_sum, z_sum = xa + xb, ya + yb, za + zb
    jx, jy, jz = d[1] + x_sum, d[3] + y_sum, d[5] + z_sum
    xx, yy, zz = jx * jx, jy * jy, jz * jz
    yz_sum = yy + zz
    jj = xx + yz_sum
    e1 = (1.19 * 19.0 / 2394.0) * ((across - f[0]) - jj)
    e2 = (1.4 / 252.0) * ((9.0 * f[0] - 7.0 * along) - (2.0 * across - 5.5 * jj))
    qx = (1.2 / 40.0 * 5.0 / 3.0) * (x_sum - 2.0 * d[1])
    qy = (1.2 / 40.0 * 5.0 / 3.0) * (y_sum - 2.0 * d[3])
    qz = (1.2 / 40.0 * 5.0 / 3.0) * (z_sum - 2.0 * d[5])
    axial = (2.0 * sx) - (sy + sz)
    planar = (sxy + sxz) - 2.0 * syz
    stress = 2.0 * xx - yz_sum
    e9 = (shear * (1.0 / 36.0)) * ((axial + planar) - stress)
    e10 = (1.4 / 72.0) * ((planar - 2.0 * axial) + 0.5 * stress)
    axial_w = sy - sz
    planar_w = sxy - sxz
    stress_w = yy - zz
    e11 = (shear * (1.0 / 12.0)) * ((axial_w + planar_w) - stress_w)
    e12 = (1.4 / 24.0) * ((planar_w - 2.0 * axial_w) + 0.5 * stress_w)
    quarter = shear * 0.25
    e13 = quarter * ((s[7] - s[9]) - jx * jy)
    e14 = quarter * ((s[15] - s[17]) - jy * jz)
    e15 = quarter * ((s[11] - s[13]) - jx * jz)
    e16 = (1.98 / 8.0) * (xa - xb)
    e17 = (1.98 / 8.0) * (ya - yb)
    e18 = (1.98 / 8.0) * (za - zb)
    post = [None] * 19
    post[0] = f[0] + (30.0 * e1 - 12.0 * e2)
    base = 11.0 * e1 + 4.0 * e2
    t9 = e9 - 2.0 * e10
    t11 = e11 - 2.0 * e12
    evens = {1: 2.0 * t9 - base, 3: t11 - (t9 + base), 5: -((t11 + t9) + base)}
    base = 8.0 * e1 + e2
    u9 = e9 + e10
    u11 = e11 + e12
    upper, lower, third = base + u9 + u11, base + u9 - u11, base - 2.0 * u9
    evens.update({7: upper + e13, 9: upper - e13, 11: lower + e15, 13: lower - e15, 15: third + e14, 17: third - e14})
    xp, xm = qx + e16, qx - e16
    yp, ym = qy + e17, qy - e17
    zp, zm = qz + e18, qz - e18
    odds = {
        1: -4.0 * qx, 3: -4.0 * qy, 5: -4.0 * qz,
        7: xp + ym, 9: xp - ym, 11: xm + zp, 13: xm - zp, 15: yp + zm, 17: yp - zm,
    }
    for q in range(1, 19, 2):
        post[q] = f[q] - (evens[q] + odds[q])
        post[q + 1] = f[q + 1] - (evens[q] - odds[q])
    return post


def arrived(q, v, post, halo):
    _, lane = grid_iotas()
    cx, cy, cz = VELOCITY[q]
    start = TOP + 8 * v - 2 * cx
    value = post[q, start : start + 8, :]
    by = 16 * cy + cz
    if cy != 0:
        beside = post[q, start - cy : start - cy + 8, :]
        value = jnp.where(lane >= 128 - by if cy == 1 else lane < -by, beside, value)
    value = turned(value, by)
    masks = [m for m in outside(q, v) if m is not None]
    if masks:
        edge = halo[q, 8 * v : 8 * v + 8, :]
        bounced = post[OPPOSITE[q], TOP + 8 * v : TOP + 8 * v + 8, :]
        value = jnp.where(functools.reduce(jnp.logical_or, masks), jnp.where(edge < 0.0, bounced, edge), value)
    return value


def collide_first(first, post, shear):
    for v in range(4):
        values = collide([first[q, 8 * v : 8 * v + 8, :] for q in range(19)], shear)
        for q in range(19):
            post[q, TOP + 8 * v : TOP + 8 * v + 8, :] = values[q]


def run_and_collide(state, post, target, halo, shear):
    for v in range(4):
        values = [arrived(q, v, post, halo) for q in range(19)]
        for q in range(19):
            state[q, 8 * v : 8 * v + 8, :] = values[q]
        values = collide(values, shear)
        for q in range(19):
            target[q, TOP + 8 * v : TOP + 8 * v + 8, :] = values[q]


def run_last(state, post, halo):
    for v in range(4):
        for q in range(19):
            state[q, 8 * v : 8 * v + 8, :] = arrived(q, v, post, halo)


def kernel(
    sizes, pop, plan_in, out, ids, raw, plan, theirs, state, cube, packets, gone, interface_out, first, interface, planes, post, halo,
    load_sem, send_sem, recv_sem, answer_sem, near_sem, across_sem,
):
    ny, nz, total = sizes
    bit = ny * nz
    me = lax.axis_index("gx") * bit + lax.axis_index("gy") * nz + lax.axis_index("gz")

    def place(d):
        return (d // bit, d // nz % ny, d % nz)

    partner_id = lax.rem(me // bit, 2) * (-2 * bit) + bit + me
    partner = place(partner_id)
    later = place(lax.rem(me + 1, total))
    before = place(lax.rem(me + total - 1, total))

    loads = [
        pltpu.make_async_copy(source, target, load_sem.at[k]) for k, (source, target) in enumerate(((plan_in, plan), (pop, raw)))
    ]
    for load in loads:
        load.start()

    odd = lax.rem(me // bit, 2) == 1
    inner = lax.rem(me, bit)
    at_start, at_end = inner == 0, inner == bit - 1
    even = jnp.logical_not(odd)
    barrier = pltpu.get_barrier_semaphore()

    def signal(semaphore, device):
        pl.semaphore_signal(semaphore, inc=1, device_id=device, device_id_type=MESH)

    @pl.when(odd)
    def _():
        signal(barrier, partner)

    @pl.when(even & at_start)
    def _():
        signal(barrier, before)

    @pl.when(even & at_end)
    def _():
        signal(barrier, later)

    def remote(source, target, number, device):
        return pltpu.make_async_remote_copy(
            src_ref=source,
            dst_ref=target,
            send_sem=send_sem.at[number],
            recv_sem=recv_sem.at[number],
            device_id=device,
            device_id_type=MESH,
        )

    @pl.when(even)
    def _():
        pl.semaphore_wait(barrier, 1)
        signal(answer_sem, partner)

    @pl.when(odd)
    def _():
        pl.semaphore_wait(answer_sem, 1)

    @pl.when(odd & jnp.logical_not(at_start))
    def _():
        signal(barrier, before)

    @pl.when(odd & jnp.logical_not(at_end))
    def _():
        signal(barrier, later)

    for load in loads:
        load.wait()

    moved = [plan[5, 0], plan[5, 1]]
    for k in range(2):
        for q in range(19):
            for v in range(4):
                gone[k, q, 8 * v : 8 * v + 8, :] = raw[q, pl.ds(32 * v + moved[k], 8, stride=4), :]

    orders = remote(plan, theirs, 12, partner)
    orders.start()
    blocks = [remote(gone.at[k], first.at[2 + k], k, partner) for k in range(2)]
    for copy in blocks:
        copy.start()

    @pl.when(odd)
    def _():
        pl.semaphore_wait(barrier, 2)
        signal(near_sem, partner)

    @pl.when(odd & at_start)
    def _():
        signal(across_sem, before)

    @pl.when(odd & at_end)
    def _():
        signal(across_sem, later)

    for b in range(4):
        unpacked(raw, cube, b)

    pack_faces(cube, packets, 0, 4)

    @pl.when(even)
    def _():
        pl.semaphore_wait(near_sem, 1)

    @pl.when(even & (at_start | at_end))
    def _():
        pl.semaphore_wait(across_sem, 1)

    halos = []
    for b in range(4):
        if b > 0:
            pack_faces(cube, packets, b, 4 + b)
        for number, at, device in ((4 + b, b, later), (8 + b, 8 + b, before)):
            copy = remote(packets.at[4 + b], packets.at[at], number, device)
            copy.start()
            halos.append(copy)
    low = jnp.minimum(moved[0], moved[1])
    high = jnp.maximum(moved[0], moved[1])
    stay0 = jnp.where(low > 0, 0, jnp.where(high > 1, 1, 2))
    stay1 = jnp.minimum(6 - low - high - stay0, 3)

    def keep(j, carry):
        stay = jnp.where(j == 0, stay0, stay1)

        def one(q, inner_carry):
            first[j, q] = cube[stay, q, TOP : TOP + 32, :]
            return inner_carry

        lax.fori_loop(0, 19, one, 0)
        count = jnp.full((8, 128), plan[4, stay], jnp.int32).astype(jnp.float32)
        collide_first(first.at[j], post.at[j, 0], 1.0 / (count * (1.0 / 1.6 - 0.5) + 0.5))
        return carry

    lax.fori_loop(0, 2, keep, 0)

    for copy in halos:
        copy.wait_recv()

    lowest = (me - 1) * 4
    faces = []
    for k in range(2):
        assemble(packets, plan, moved[k], lowest, interface_out, k, moved[k])
        copy = remote(interface_out.at[k], interface.at[2 + k], 2 + k, partner)
        copy.start()
        faces.append(copy)

    for j, stay in enumerate((stay0, stay1)):
        assemble(packets, plan, stay, lowest, interface, j, stay)

    def job(j, carry):
        for k in range(2):
            @pl.when(j == 2 + k)
            def _(k=k):
                faces[k].wait_recv()
                blocks[k].wait_recv()

        count = jnp.broadcast_to(interface[j, COUNT_ROW : COUNT_ROW + 1, :], (8, 128))
        shear = 1.0 / (count * (1.0 / 1.6 - 0.5) + 0.5)
        spread(interface, j, planes)
        build_halo(planes, halo)

        @pl.when(j >= 2)
        def _():
            collide_first(first.at[j], post.at[j, 0], shear)

        def one(step, inner_carry):
            now = lax.rem(step, 2)
            run_and_collide(state.at[step, j], post.at[j, now], post.at[j, 1 - now], halo, shear)
            return inner_carry

        lax.fori_loop(0, 3, one, 0)
        run_last(state.at[3, j], post.at[j, 1], halo)
        return carry

    lax.fori_loop(0, 4, job, 0)

    orders.wait_recv()
    for s in range(4):
        here = jnp.where(moved[0] == s, 2, jnp.where(moved[1] == s, 3, jnp.where(stay0 == s, 0, 1)))
        sent = jnp.where(moved[0] == s, theirs[5, 0], theirs[5, 1])
        foreign = here >= 2
        count = jnp.where(foreign, theirs[4, jnp.clip(sent, 0, 3)], plan[4, s])
        step = jnp.clip(count - 1, 0, 3)
        for q in range(19):
            for v in range(4):
                out[q, pl.ds(32 * v + s, 8, stride=4), :] = state[step, here, q, 8 * v : 8 * v + 8, :]
        ids[s] = jnp.where(foreign, partner_id * 4 + sent, me * 4 + s)

    for copy in halos + blocks + faces + [orders]:
        copy.wait_send()


def write(result, ids_in, out, ids, sems):
    copies = [pltpu.make_async_copy(result, out, sems.at[0]), pltpu.make_async_copy(ids_in, ids, sems.at[1])]
    for copy in copies:
        copy.start()
    for copy in copies:
        copy.wait()


def shards(sizes, populations, neighbours, substeps, moves):
    f32 = jnp.float32
    lying = populations.reshape(4, 19, 32, 128).transpose(1, 2, 0, 3).reshape(19, 128, 128)
    plan = jnp.concatenate(
        [neighbours, jnp.pad(substeps[None], ((0, 0), (0, 2))), jnp.pad(moves, ((0, 0), (0, 4)))], axis=0
    )
    vmem, smem = pl.BlockSpec(memory_space=pltpu.VMEM), pl.BlockSpec(memory_space=pltpu.SMEM)
    whole = pl.BlockSpec(memory_space=pl.ANY)
    shapes = (jax.ShapeDtypeStruct((19, 128, 128), f32), jax.ShapeDtypeStruct((4,), jnp.int32))
    result, ids = pl.pallas_call(
        functools.partial(kernel, sizes),
        out_shape=shapes,
        in_specs=[whole, whole],
        out_specs=(vmem, smem),
        scratch_shapes=[
            pltpu.VMEM((19, 128, 128), f32),
            pltpu.SMEM((6, 6), jnp.int32),
            pltpu.SMEM((6, 6), jnp.int32),
            pltpu.VMEM((4, 4, 19, 32, 128), f32),
            pltpu.VMEM((4, 19, 48, 128), f32),
            pltpu.VMEM((12, SENT_ROWS, 128), f32),
            pltpu.VMEM((2, 19, 32, 128), f32),
            pltpu.VMEM((2, SENT_ROWS, 128), f32),
            pltpu.VMEM((4, 19, 32, 128), f32),
            pltpu.VMEM((4, SENT_ROWS, 128), f32),
            pltpu.VMEM((PLANE_ROWS, 128), f32),
            pltpu.VMEM((4, 2, 19, 48, 128), f32),
            pltpu.VMEM((19, 32, 128), f32),
            pltpu.SemaphoreType.DMA((2,)),
            pltpu.SemaphoreType.DMA((13,)),
            pltpu.SemaphoreType.DMA((13,)),
            pltpu.SemaphoreType.REGULAR,
            pltpu.SemaphoreType.REGULAR,
            pltpu.SemaphoreType.REGULAR,
        ],
        compiler_params=pltpu.CompilerParams(
            collective_id=0, has_side_effects=True, vmem_limit_bytes=53500 * 1024
        ),
        name="lattice_step",
    )(lying, plan)
    result, ids = pl.pallas_call(
        write,
        out_shape=shapes,
        in_specs=[vmem, whole],
        out_specs=(whole, whole),
        scratch_shapes=[pltpu.SemaphoreType.DMA((2,))],
        compiler_params=pltpu.CompilerParams(vmem_limit_bytes=36 * 1024 * 1024),
        name="write_out",
    )(result, ids)
    return result.reshape(19, 32, 4, 128).transpose(2, 0, 1, 3).reshape(4, 19, 4096), ids


def solution(mesh):
    sizes = (mesh.shape["gy"], mesh.shape["gz"], mesh.size)
    return jax.shard_map(
        functools.partial(shards, sizes),
        mesh=mesh,
        in_specs=(P(AXES, None, None), P(AXES, None), P(AXES), P(AXES, None)),
        out_specs=(P(AXES, None, None), P(AXES)),
        check_vma=False,
    )
```

```python
import functools

import jax
import jax.numpy as jnp
import numpy as np
from jax import lax
from jax.experimental import pallas as pl
from jax.experimental.pallas import tpu as pltpu
from jax.sharding import PartitionSpec as P

MESH = pl.DeviceIdType.MESH
AXES = ("gx", "gy", "gz")
VELOCITY = [
    (0, 0, 0), (1, 0, 0), (-1, 0, 0), (0, 1, 0), (0, -1, 0), (0, 0, 1), (0, 0, -1),
    (1, 1, 0), (-1, -1, 0), (1, -1, 0), (-1, 1, 0), (1, 0, 1), (-1, 0, -1),
    (1, 0, -1), (-1, 0, 1), (0, 1, 1), (0, -1, -1), (0, 1, -1), (0, -1, 1),
]
OPPOSITE = [0, 2, 1, 4, 3, 6, 5, 8, 7, 10, 9, 12, 11, 14, 13, 16, 15, 18, 17]
LEAVING = [
    [2, 8, 10, 12, 14], [1, 7, 9, 11, 13], [4, 8, 9, 16, 18],
    [3, 7, 10, 15, 17], [6, 12, 13, 16, 17], [5, 11, 14, 15, 18],
]
Y_SENT, Z_SENT, X_SENT, SENT_ROWS = 0, 24, 48, 64
X_ROW, Y_ROW, Z_ROW, PLANE_ROWS = 0, 24, 56, 96
TOP = 8


def turned(value, by):
    by = by % 128
    return value if by == 0 else pltpu.roll(value, by, 1)


def grid_iotas():
    row = lax.broadcasted_iota(jnp.int32, (8, 128), 0)
    lane = lax.broadcasted_iota(jnp.int32, (8, 128), 1)
    return row, lane


def unpacked(raw, cube, block):
    for q in range(19):
        for v in range(4):
            cube[block, q, TOP + 8 * v : TOP + 8 * v + 8, :] = raw[q, pl.ds(32 * v + block, 8, stride=4), :]


def pack_faces(cube, packets, block, slot, corner):
    row, lane = grid_iotas()
    even = row % 2 == 0
    place = (lane // 16 - row % 2) % 8
    for face in range(2):
        start = TOP if face == 0 else TOP + 30
        for k in range(5):
            at = 10 * face + 2 * k
            pair = cube[block, LEAVING[face][k], start : start + 2, :]
            if at < 16:
                packets[slot, X_SENT + at : X_SENT + at + 2, :] = pair
            else:
                corner[at - 16 : at - 14, :] = pair
                corner[at - 12 : at - 10, :] = pair
    ys, zs = [], []
    for v in range(4):
        base = TOP + 8 * v
        kept = jnp.zeros((8, 128), jnp.float32)
        for k in range(5):
            far = cube[block, LEAVING[3][k], base + 1 : base + 9, :]
            near = cube[block, LEAVING[2][k], base - 1 : base + 7, :]
            moved = turned(jnp.where(even, far, near), 16 * (k + 1))
            kept = jnp.where(place == k, moved, kept)
        ys.append(kept)
        kept = jnp.zeros((8, 128), jnp.float32)
        for k in range(5):
            near = cube[block, LEAVING[4][k], base : base + 8, :]
            far = cube[block, LEAVING[5][k], base : base + 8, :]
            moved = turned(jnp.where(lane % 16 == 15, far, near), 2 * k + 1)
            kept = jnp.where(lane % 16 // 2 == k, moved, kept)
        zs.append(kept)
    ys[0] = jnp.where(place >= 5, turned(ys[3], 80), ys[0])
    ys[1] = jnp.where(place >= 5, turned(ys[3], 32), ys[1])
    zs[0] = jnp.where(lane % 16 >= 10, turned(zs[3], 10), zs[0])
    zs[1] = jnp.where(lane % 16 >= 10, turned(zs[3], 4), zs[1])
    rest = corner[...]
    rest = jnp.where(row < 4, rest, turned(rest, 64))
    ys[1] = jnp.where(place == 7, jnp.where(even, turned(rest, 64), turned(rest, 80)), ys[1])
    ys[2] = jnp.where(place >= 5, jnp.where(even, turned(rest, 80), turned(rest, 96)), ys[2])
    for v in range(3):
        packets[slot, Y_SENT + 8 * v : Y_SENT + 8 * v + 8, :] = ys[v]
        packets[slot, Z_SENT + 8 * v : Z_SENT + 8 * v + 8, :] = zs[v]


def spread(sent, slot, planes):
    row, lane = grid_iotas()
    place = (lane // 16 - row % 2) % 8
    ys = [sent[slot, Y_SENT + 8 * v : Y_SENT + 8 * v + 8, :] for v in range(3)]
    zs = [sent[slot, Z_SENT + 8 * v : Z_SENT + 8 * v + 8, :] for v in range(3)]
    ys.append(jnp.where(place < 3, turned(ys[0], -80), turned(ys[1], -32)))
    zs.append(jnp.where(lane % 16 < 6, turned(zs[0], -10), turned(zs[1], -4)))
    for v in range(4):
        planes[Y_ROW + 8 * v : Y_ROW + 8 * v + 8, :] = ys[v]
        planes[Z_ROW + 8 * v : Z_ROW + 8 * v + 8, :] = zs[v]
    for v in range(2):
        planes[X_ROW + 8 * v : X_ROW + 8 * v + 8, :] = sent[slot, X_SENT + 8 * v : X_SENT + 8 * v + 8, :]
    even = row % 2 == 0
    one = jnp.where(even, turned(ys[1], -64), turned(ys[1], -80))
    rest = jnp.where(lane // 16 == 3, one, jnp.where(even, turned(ys[2], -80), turned(ys[2], -96)))
    planes[X_ROW + 16 : X_ROW + 24, :] = rest
    below = turned(planes[X_ROW + 20 : X_ROW + 28, :], 64)
    planes[X_ROW + 16 : X_ROW + 20, :] = jnp.where(lane < 64, rest, below)[0:4]


def assemble(packets, plan, block, first, out, slot):
    row, lane = grid_iotas()
    at, valid = [], []
    for face in range(6):
        near = plan[block, face]
        valid.append(jnp.full((8, 128), near, jnp.int32) >= 0)
        at.append(jnp.clip(near - first, 0, 11))
    place = (lane // 16 - row % 2) % 8
    upper, lower = slice(X_SENT, X_SENT + 8), slice(X_SENT + 8, X_SENT + 16)
    out[slot, upper, :] = jnp.where(valid[1], packets[at[1], upper, :], -1.0)
    second = jnp.where(valid[1], packets[at[1], lower, :], -1.0)
    out[slot, lower, :] = jnp.where(row < 2, second, jnp.where(valid[0], packets[at[0], lower, :], -1.0))
    for v in range(3):
        rows = slice(Y_SENT + 8 * v, Y_SENT + 8 * v + 8)
        even_rows = jnp.where(valid[2], packets[at[2], rows, :], -1.0)
        odd_rows = jnp.where(valid[3], packets[at[3], rows, :], -1.0)
        value = jnp.where(row % 2 == 0, even_rows, odd_rows)
        if v > 0:
            value = jnp.where(place >= (7 if v == 1 else 5), jnp.where(valid[0], packets[at[0], rows, :], -1.0), value)
        out[slot, rows, :] = value
        rows = slice(Z_SENT + 8 * v, Z_SENT + 8 * v + 8)
        low = jnp.where(valid[4], packets[at[4], rows, :], -1.0)
        high = jnp.where(valid[5], packets[at[5], rows, :], -1.0)
        out[slot, rows, :] = jnp.where(lane % 2 == 0, low, high)


def outside(which, v):
    row, lane = grid_iotas()
    cx, cy, cz = VELOCITY[which]
    x_mask = y_mask = z_mask = None
    if cx == 1 and v == 0:
        x_mask = row < 2
    if cx == -1 and v == 3:
        x_mask = row >= 6
    if cy == 1:
        y_mask = (row % 2 == 0) & (lane < 16)
    if cy == -1:
        y_mask = (row % 2 == 1) & (lane >= 112)
    if cz == 1:
        z_mask = lane % 16 == 0
    if cz == -1:
        z_mask = lane % 16 == 15
    return x_mask, y_mask, z_mask


def build_halo(planes, halo):
    row, lane = grid_iotas()
    for which in range(1, 19):
        cx, cy, cz = VELOCITY[which]
        for v in range(4):
            x_mask, y_mask, z_mask = outside(which, v)
            value = None
            if z_mask is not None:
                face = 4 if cz == 1 else 5
                k = LEAVING[face ^ 1].index(which)
                by = 16 * cy - (2 * k + 1) + (-15 if cz == 1 else 15)
                start = Z_ROW + 8 * v - 2 * cx
                value = planes[start : start + 8, :]
                if cy != 0:
                    beside = planes[start - cy : start - cy + 8, :]
                    to = (lane + by) % 128
                    value = jnp.where(to < 16 if cy == 1 else to >= 112, beside, value)
                value = turned(value, by)
            if y_mask is not None:
                face = 2 if cy == 1 else 3
                k = LEAVING[face ^ 1].index(which)
                by = -16 * k if cy == 1 else 112 - 16 * (k + 1)
                start = Y_ROW + 8 * v - 2 * cx
                plane = planes[start : start + 8, :]
                line = turned(plane, by)
                if cz != 0:
                    line = jnp.where(lane % 16 == (0 if cz == 1 else 15), line, turned(plane, by + cz))
                value = line if value is None else jnp.where(y_mask, line, value)
            if x_mask is not None:
                face = 0 if cx == 1 else 1
                k = LEAVING[face ^ 1].index(which)
                at = X_ROW + 10 * (face ^ 1) + 2 * k
                pair = planes[at : at + 2, :]
                upper, lower = pair[0:1], pair[1:2]
                if cy == 1:
                    high, low = turned(upper, 16), turned(lower, 16)
                    lane1 = lane[0:1]
                    lower = jnp.where(lane1 < 16, high, low)
                    upper = jnp.where(lane1 < 16, upper, high)
                elif cy == -1:
                    high, low = turned(upper, -16), turned(lower, -16)
                    lane1 = lane[0:1]
                    upper = jnp.where(lane1 >= 112, low, high)
                    lower = jnp.where(lane1 >= 112, lower, low)
                elif cz != 0:
                    edge = lane[0:1] % 16 == (0 if cz == 1 else 15)
                    upper = jnp.where(edge, upper, turned(upper, cz))
                    lower = jnp.where(edge, lower, turned(lower, cz))
                both = jnp.where(
                    row % 2 == 0,
                    jnp.broadcast_to(upper, (8, 128)),
                    jnp.broadcast_to(lower, (8, 128)),
                )
                value = both if value is None else jnp.where(x_mask, both, value)
            if value is not None:
                halo[which, 8 * v : 8 * v + 8, :] = value


def collide(f, shear):
    s = {q: f[q] + f[q + 1] for q in range(1, 19, 2)}
    d = {q: f[q] - f[q + 1] for q in range(1, 19, 2)}
    sx, sy, sz = s[1], s[3], s[5]
    sxy, sxz, syz = s[7] + s[9], s[11] + s[13], s[15] + s[17]
    along = sx + (sy + sz)
    across = sxy + (sxz + syz)
    xa, xb = d[7] + d[9], d[11] + d[13]
    ya, yb = d[15] + d[17], d[7] - d[9]
    za, zb = d[11] - d[13], d[15] - d[17]
    x_sum, y_sum, z_sum = xa + xb, ya + yb, za + zb
    jx, jy, jz = d[1] + x_sum, d[3] + y_sum, d[5] + z_sum
    xx, yy, zz = jx * jx, jy * jy, jz * jz
    yz_sum = yy + zz
    jj = xx + yz_sum
    e1 = (1.19 * 19.0 / 2394.0) * ((across - f[0]) - jj)
    e2 = (1.4 / 252.0) * ((9.0 * f[0] - 7.0 * along) - (2.0 * across - 5.5 * jj))
    qx = (1.2 / 40.0 * 5.0 / 3.0) * (x_sum - 2.0 * d[1])
    qy = (1.2 / 40.0 * 5.0 / 3.0) * (y_sum - 2.0 * d[3])
    qz = (1.2 / 40.0 * 5.0 / 3.0) * (z_sum - 2.0 * d[5])
    axial = (2.0 * sx) - (sy + sz)
    planar = (sxy + sxz) - 2.0 * syz
    stress = 2.0 * xx - yz_sum
    e9 = (shear * (1.0 / 36.0)) * ((axial + planar) - stress)
    e10 = (1.4 / 72.0) * ((planar - 2.0 * axial) + 0.5 * stress)
    axial_w = sy - sz
    planar_w = sxy - sxz
    stress_w = yy - zz
    e11 = (shear * (1.0 / 12.0)) * ((axial_w + planar_w) - stress_w)
    e12 = (1.4 / 24.0) * ((planar_w - 2.0 * axial_w) + 0.5 * stress_w)
    quarter = shear * 0.25
    e13 = quarter * ((s[7] - s[9]) - jx * jy)
    e14 = quarter * ((s[15] - s[17]) - jy * jz)
    e15 = quarter * ((s[11] - s[13]) - jx * jz)
    e16 = (1.98 / 8.0) * (xa - xb)
    e17 = (1.98 / 8.0) * (ya - yb)
    e18 = (1.98 / 8.0) * (za - zb)
    post = [None] * 19
    post[0] = f[0] + (30.0 * e1 - 12.0 * e2)
    base = 11.0 * e1 + 4.0 * e2
    t9 = e9 - 2.0 * e10
    t11 = e11 - 2.0 * e12
    evens = {1: 2.0 * t9 - base, 3: t11 - (t9 + base), 5: -((t11 + t9) + base)}
    base = 8.0 * e1 + e2
    u9 = e9 + e10
    u11 = e11 + e12
    upper, lower, third = base + u9 + u11, base + u9 - u11, base - 2.0 * u9
    evens.update({7: upper + e13, 9: upper - e13, 11: lower + e15, 13: lower - e15, 15: third + e14, 17: third - e14})
    xp, xm = qx + e16, qx - e16
    yp, ym = qy + e17, qy - e17
    zp, zm = qz + e18, qz - e18
    odds = {
        1: -4.0 * qx, 3: -4.0 * qy, 5: -4.0 * qz,
        7: xp + ym, 9: xp - ym, 11: xm + zp, 13: xm - zp, 15: yp + zm, 17: yp - zm,
    }
    for q in range(1, 19, 2):
        post[q] = f[q] - (evens[q] + odds[q])
        post[q + 1] = f[q + 1] - (evens[q] - odds[q])
    return post


def arrived(q, v, post, halo):
    _, lane = grid_iotas()
    cx, cy, cz = VELOCITY[q]
    start = TOP + 8 * v - 2 * cx
    value = post[q, start : start + 8, :]
    by = 16 * cy + cz
    if cy != 0:
        beside = post[q, start - cy : start - cy + 8, :]
        value = jnp.where(lane >= 128 - by if cy == 1 else lane < -by, beside, value)
    value = turned(value, by)
    masks = [m for m in outside(q, v) if m is not None]
    if masks:
        edge = halo[q, 8 * v : 8 * v + 8, :]
        bounced = post[OPPOSITE[q], TOP + 8 * v : TOP + 8 * v + 8, :]
        value = jnp.where(functools.reduce(jnp.logical_or, masks), jnp.where(edge < 0.0, bounced, edge), value)
    return value


def collide_first(first, post, shear):
    for v in range(4):
        values = collide([first[q, 8 * v : 8 * v + 8, :] for q in range(19)], shear)
        for q in range(19):
            post[q, TOP + 8 * v : TOP + 8 * v + 8, :] = values[q]


def run_and_collide(state, post, target, halo, shear):
    for v in range(4):
        values = [arrived(q, v, post, halo) for q in range(19)]
        for q in range(19):
            state[q, 8 * v : 8 * v + 8, :] = values[q]
        values = collide(values, shear)
        for q in range(19):
            target[q, TOP + 8 * v : TOP + 8 * v + 8, :] = values[q]


def run_last(state, post, halo):
    for v in range(4):
        for q in range(19):
            state[q, 8 * v : 8 * v + 8, :] = arrived(q, v, post, halo)


def kernel(
    sizes, pop, plan_in, out, ids, raw, plan, theirs, state, cube, packets, gone, interface_out, first, interface, planes, corner, post, halo,
    load_sem, send_sem, recv_sem, answer_sem, near_sem, across_sem,
):
    ny, nz, total = sizes
    bit = ny * nz
    me = lax.axis_index("gx") * bit + lax.axis_index("gy") * nz + lax.axis_index("gz")

    def place(d):
        return (d // bit, d // nz % ny, d % nz)

    partner_id = lax.rem(me // bit, 2) * (-2 * bit) + bit + me
    partner = place(partner_id)
    later = place(lax.rem(me + 1, total))
    before = place(lax.rem(me + total - 1, total))

    loads = [
        pltpu.make_async_copy(source, target, load_sem.at[k]) for k, (source, target) in enumerate(((plan_in, plan), (pop, raw)))
    ]
    for load in loads:
        load.start()

    odd = lax.rem(me // bit, 2) == 1
    inner = lax.rem(me, bit)
    at_start, at_end = inner == 0, inner == bit - 1
    even = jnp.logical_not(odd)
    barrier = pltpu.get_barrier_semaphore()

    def signal(semaphore, device):
        pl.semaphore_signal(semaphore, inc=1, device_id=device, device_id_type=MESH)

    @pl.when(odd)
    def _():
        signal(barrier, partner)

    @pl.when(even & at_start)
    def _():
        signal(barrier, before)

    @pl.when(even & at_end)
    def _():
        signal(barrier, later)

    def remote(source, target, number, device):
        return pltpu.make_async_remote_copy(
            src_ref=source,
            dst_ref=target,
            send_sem=send_sem.at[number],
            recv_sem=recv_sem.at[number],
            device_id=device,
            device_id_type=MESH,
        )

    @pl.when(even)
    def _():
        pl.semaphore_wait(barrier, 1)
        signal(answer_sem, partner)

    @pl.when(odd)
    def _():
        pl.semaphore_wait(answer_sem, 1)

    @pl.when(odd & jnp.logical_not(at_start))
    def _():
        signal(barrier, before)

    @pl.when(odd & jnp.logical_not(at_end))
    def _():
        signal(barrier, later)

    for load in loads:
        load.wait()

    moved = [plan[5, 0], plan[5, 1]]
    for k in range(2):
        for q in range(19):
            for v in range(4):
                gone[k, q, 8 * v : 8 * v + 8, :] = raw[q, pl.ds(32 * v + moved[k], 8, stride=4), :]

    orders = remote(plan, theirs, 12, partner)
    orders.start()
    blocks = [remote(gone.at[k], first.at[2 + k], k, partner) for k in range(2)]
    for copy in blocks:
        copy.start()

    @pl.when(odd)
    def _():
        pl.semaphore_wait(barrier, 2)
        signal(near_sem, partner)

    @pl.when(odd & at_start)
    def _():
        signal(across_sem, before)

    @pl.when(odd & at_end)
    def _():
        signal(across_sem, later)

    for b in range(4):
        unpacked(raw, cube, b)

    pack_faces(cube, packets, 0, 4, corner)

    @pl.when(even)
    def _():
        pl.semaphore_wait(near_sem, 1)

    @pl.when(even & (at_start | at_end))
    def _():
        pl.semaphore_wait(across_sem, 1)

    gz = lax.rem(me, nz)
    far_later = (gz == nz // 2 - 1) | (gz == nz - 1)
    far_before = (gz == nz // 2) | (gz == 0)
    early = (far_later | far_before) & (gz < nz // 2) & (lax.rem(me // nz, ny) // 2 < ny // 4)
    halos = []
    for b in range(4):
        if b > 0:
            pack_faces(cube, packets, b, 4 + b, corner)
        for number, at, device, far in ((4 + b, b, later, far_later), (8 + b, 8 + b, before, far_before)):
            copy = remote(packets.at[4 + b], packets.at[at], number, device)
            pl.when(far)(copy.start)
            halos.append((copy, far))
    for copy, far in halos:
        pl.when(jnp.logical_not(far))(copy.start)

    low = jnp.minimum(moved[0], moved[1])
    high = jnp.maximum(moved[0], moved[1])
    stay0 = jnp.where(low > 0, 0, jnp.where(high > 1, 1, 2))
    stay1 = jnp.minimum(6 - low - high - stay0, 3)

    def keep(j, carry):
        stay = jnp.where(j == 0, stay0, stay1)

        def one(q, inner_carry):
            first[j, q] = cube[stay, q, TOP : TOP + 32, :]
            return inner_carry

        lax.fori_loop(0, 19, one, 0)
        count = jnp.full((8, 128), plan[4, stay], jnp.int32).astype(jnp.float32)
        collide_first(first.at[j], post.at[j, 0], 1.0 / (count * (1.0 / 1.6 - 0.5) + 0.5))
        return carry

    lax.fori_loop(0, 2, keep, 0)

    orders.wait_recv()

    def shear_of(j):
        came = theirs[4, jnp.clip(theirs[5, jnp.clip(j - 2, 0, 1)], 0, 3)]
        count = jnp.where(j == 0, plan[4, stay0], jnp.where(j == 1, plan[4, stay1], came))
        return 1.0 / (jnp.full((8, 128), count, jnp.int32).astype(jnp.float32) * (1.0 / 1.6 - 0.5) + 0.5)

    def start_foreign():
        for copy in blocks:
            copy.wait_recv()

        def one(j, carry):
            collide_first(first.at[j], post.at[j, 0], shear_of(j))
            return carry

        lax.fori_loop(2, 4, one, 0)

    pl.when(early)(start_foreign)

    for copy, _ in halos:
        copy.wait_recv()

    lowest = (me - 1) * 4
    faces = []
    for k in range(2):
        assemble(packets, plan, moved[k], lowest, interface_out, k)
        copy = remote(interface_out.at[k], interface.at[2 + k], 2 + k, partner)
        copy.start()
        faces.append(copy)

    for j, stay in enumerate((stay0, stay1)):
        assemble(packets, plan, stay, lowest, interface, j)

    def job(j, carry):
        for k in range(2):
            @pl.when(j == 2 + k)
            def _(k=k):
                faces[k].wait_recv()

        pl.when((j == 2) & jnp.logical_not(early))(start_foreign)
        shear = shear_of(j)
        spread(interface, j, planes)
        build_halo(planes, halo)

        def one(step, inner_carry):
            now = lax.rem(step, 2)
            run_and_collide(state.at[step, j], post.at[j, now], post.at[j, 1 - now], halo, shear)
            return inner_carry

        lax.fori_loop(0, 3, one, 0)
        run_last(state.at[3, j], post.at[j, 1], halo)
        return carry

    lax.fori_loop(0, 4, job, 0)

    for s in range(4):
        here = jnp.where(moved[0] == s, 2, jnp.where(moved[1] == s, 3, jnp.where(stay0 == s, 0, 1)))
        sent = jnp.where(moved[0] == s, theirs[5, 0], theirs[5, 1])
        foreign = here >= 2
        count = jnp.where(foreign, theirs[4, jnp.clip(sent, 0, 3)], plan[4, s])
        step = jnp.clip(count - 1, 0, 3)
        for q in range(19):
            for v in range(4):
                out[q, pl.ds(32 * v + s, 8, stride=4), :] = state[step, here, q, 8 * v : 8 * v + 8, :]
        ids[s] = jnp.where(foreign, partner_id * 4 + sent, me * 4 + s)

    for copy in [copy for copy, _ in halos] + blocks + faces + [orders]:
        copy.wait_send()


def write(result, ids_in, out, ids, sems):
    copies = [pltpu.make_async_copy(ids_in, ids, sems.at[4])]
    for k, (low, count) in enumerate(((0, 5), (5, 5), (10, 5), (15, 4))):
        part = pl.ds(low, count)
        copies.append(pltpu.make_async_copy(result.at[part], out.at[part], sems.at[k]))
    for copy in copies:
        copy.start()
    for copy in copies:
        copy.wait()


def shards(sizes, populations, neighbours, substeps, moves):
    f32 = jnp.float32
    lying = populations.reshape(4, 19, 32, 128).transpose(1, 2, 0, 3).reshape(19, 128, 128)
    plan = jnp.concatenate(
        [neighbours, jnp.pad(substeps[None], ((0, 0), (0, 2))), jnp.pad(moves, ((0, 0), (0, 4)))], axis=0
    )
    vmem, smem = pl.BlockSpec(memory_space=pltpu.VMEM), pl.BlockSpec(memory_space=pltpu.SMEM)
    whole = pl.BlockSpec(memory_space=pl.ANY)
    shapes = (jax.ShapeDtypeStruct((19, 128, 128), f32), jax.ShapeDtypeStruct((4,), jnp.int32))
    result, ids = pl.pallas_call(
        functools.partial(kernel, sizes),
        out_shape=shapes,
        in_specs=[whole, whole],
        out_specs=(vmem, smem),
        scratch_shapes=[
            pltpu.VMEM((19, 128, 128), f32),
            pltpu.SMEM((6, 6), jnp.int32),
            pltpu.SMEM((6, 6), jnp.int32),
            pltpu.VMEM((4, 4, 19, 32, 128), f32),
            pltpu.VMEM((4, 19, 48, 128), f32),
            pltpu.VMEM((12, SENT_ROWS, 128), f32),
            pltpu.VMEM((2, 19, 32, 128), f32),
            pltpu.VMEM((2, SENT_ROWS, 128), f32),
            pltpu.VMEM((4, 19, 32, 128), f32),
            pltpu.VMEM((4, SENT_ROWS, 128), f32),
            pltpu.VMEM((PLANE_ROWS, 128), f32),
            pltpu.VMEM((8, 128), f32),
            pltpu.VMEM((4, 2, 19, 48, 128), f32),
            pltpu.VMEM((19, 32, 128), f32),
            pltpu.SemaphoreType.DMA((2,)),
            pltpu.SemaphoreType.DMA((13,)),
            pltpu.SemaphoreType.DMA((13,)),
            pltpu.SemaphoreType.REGULAR,
            pltpu.SemaphoreType.REGULAR,
            pltpu.SemaphoreType.REGULAR,
        ],
        compiler_params=pltpu.CompilerParams(
            collective_id=0, has_side_effects=True, vmem_limit_bytes=53500 * 1024
        ),
        name="lattice_step",
    )(lying, plan)
    result, ids = pl.pallas_call(
        write,
        out_shape=shapes,
        in_specs=[vmem, whole],
        out_specs=(whole, whole),
        scratch_shapes=[pltpu.SemaphoreType.DMA((5,))],
        compiler_params=pltpu.CompilerParams(vmem_limit_bytes=36 * 1024 * 1024),
        name="write_out",
    )(result, ids)
    return result.reshape(19, 32, 4, 128).transpose(2, 0, 1, 3).reshape(4, 19, 4096), ids


def solution(mesh):
    sizes = (mesh.shape["gy"], mesh.shape["gz"], mesh.size)
    return jax.shard_map(
        functools.partial(shards, sizes),
        mesh=mesh,
        in_specs=(P(AXES, None, None), P(AXES, None), P(AXES), P(AXES, None)),
        out_specs=(P(AXES, None, None), P(AXES)),
        check_vma=False,
    )
```

```python
import functools

import jax
import jax.numpy as jnp
import numpy as np
from jax import lax
from jax.experimental import pallas as pl
from jax.experimental.pallas import tpu as pltpu
from jax.sharding import PartitionSpec as P

MESH = pl.DeviceIdType.MESH
AXES = ("gx", "gy", "gz")
VELOCITY = [
    (0, 0, 0), (1, 0, 0), (-1, 0, 0), (0, 1, 0), (0, -1, 0), (0, 0, 1), (0, 0, -1),
    (1, 1, 0), (-1, -1, 0), (1, -1, 0), (-1, 1, 0), (1, 0, 1), (-1, 0, -1),
    (1, 0, -1), (-1, 0, 1), (0, 1, 1), (0, -1, -1), (0, 1, -1), (0, -1, 1),
]
OPPOSITE = [0, 2, 1, 4, 3, 6, 5, 8, 7, 10, 9, 12, 11, 14, 13, 16, 15, 18, 17]
LEAVING = [
    [2, 8, 10, 12, 14], [1, 7, 9, 11, 13], [4, 8, 9, 16, 18],
    [3, 7, 10, 15, 17], [6, 12, 13, 16, 17], [5, 11, 14, 15, 18],
]
Y_SENT, Z_SENT, X_SENT, SENT_ROWS = 0, 24, 48, 64
X_ROW, Y_ROW, Z_ROW, PLANE_ROWS = 0, 24, 56, 96
TOP = 8


def turned(value, by):
    by = by % 128
    return value if by == 0 else pltpu.roll(value, by, 1)


def grid_iotas():
    row = lax.broadcasted_iota(jnp.int32, (8, 128), 0)
    lane = lax.broadcasted_iota(jnp.int32, (8, 128), 1)
    return row, lane


def unpacked(raw, cube, block):
    for q in range(19):
        for v in range(4):
            cube[block, q, TOP + 8 * v : TOP + 8 * v + 8, :] = raw[q, pl.ds(32 * v + block, 8, stride=4), :]


def pack_faces(cube, packets, block, slot, corner):
    row, lane = grid_iotas()
    even = row % 2 == 0
    place = (lane // 16 - row % 2) % 8
    for face in range(2):
        start = TOP if face == 0 else TOP + 30
        for k in range(5):
            at = 10 * face + 2 * k
            pair = cube[block, LEAVING[face][k], start : start + 2, :]
            if at < 16:
                packets[slot, X_SENT + at : X_SENT + at + 2, :] = pair
            else:
                corner[at - 16 : at - 14, :] = pair
                corner[at - 12 : at - 10, :] = pair
    ys, zs = [], []
    for v in range(4):
        base = TOP + 8 * v
        kept = jnp.zeros((8, 128), jnp.float32)
        for k in range(5):
            far = cube[block, LEAVING[3][k], base + 1 : base + 9, :]
            near = cube[block, LEAVING[2][k], base - 1 : base + 7, :]
            moved = turned(jnp.where(even, far, near), 16 * (k + 1))
            kept = jnp.where(place == k, moved, kept)
        ys.append(kept)
        kept = jnp.zeros((8, 128), jnp.float32)
        for k in range(5):
            near = cube[block, LEAVING[4][k], base : base + 8, :]
            far = cube[block, LEAVING[5][k], base : base + 8, :]
            moved = turned(jnp.where(lane % 16 == 15, far, near), 2 * k + 1)
            kept = jnp.where(lane % 16 // 2 == k, moved, kept)
        zs.append(kept)
    ys[0] = jnp.where(place >= 5, turned(ys[3], 80), ys[0])
    ys[1] = jnp.where(place >= 5, turned(ys[3], 32), ys[1])
    zs[0] = jnp.where(lane % 16 >= 10, turned(zs[3], 10), zs[0])
    zs[1] = jnp.where(lane % 16 >= 10, turned(zs[3], 4), zs[1])
    rest = corner[...]
    rest = jnp.where(row < 4, rest, turned(rest, 64))
    ys[1] = jnp.where(place == 7, jnp.where(even, turned(rest, 64), turned(rest, 80)), ys[1])
    ys[2] = jnp.where(place >= 5, jnp.where(even, turned(rest, 80), turned(rest, 96)), ys[2])
    for v in range(3):
        packets[slot, Y_SENT + 8 * v : Y_SENT + 8 * v + 8, :] = ys[v]
        packets[slot, Z_SENT + 8 * v : Z_SENT + 8 * v + 8, :] = zs[v]


def spread(sent, slot, planes):
    row, lane = grid_iotas()
    place = (lane // 16 - row % 2) % 8
    ys = [sent[slot, Y_SENT + 8 * v : Y_SENT + 8 * v + 8, :] for v in range(3)]
    zs = [sent[slot, Z_SENT + 8 * v : Z_SENT + 8 * v + 8, :] for v in range(3)]
    ys.append(jnp.where(place < 3, turned(ys[0], -80), turned(ys[1], -32)))
    zs.append(jnp.where(lane % 16 < 6, turned(zs[0], -10), turned(zs[1], -4)))
    for v in range(4):
        planes[Y_ROW + 8 * v : Y_ROW + 8 * v + 8, :] = ys[v]
        planes[Z_ROW + 8 * v : Z_ROW + 8 * v + 8, :] = zs[v]
    for v in range(2):
        planes[X_ROW + 8 * v : X_ROW + 8 * v + 8, :] = sent[slot, X_SENT + 8 * v : X_SENT + 8 * v + 8, :]
    even = row % 2 == 0
    one = jnp.where(even, turned(ys[1], -64), turned(ys[1], -80))
    rest = jnp.where(lane // 16 == 3, one, jnp.where(even, turned(ys[2], -80), turned(ys[2], -96)))
    planes[X_ROW + 16 : X_ROW + 24, :] = rest
    below = turned(planes[X_ROW + 20 : X_ROW + 28, :], 64)
    planes[X_ROW + 16 : X_ROW + 20, :] = jnp.where(lane < 64, rest, below)[0:4]


def assemble(packets, nbr, block, first, out, slot):
    row, lane = grid_iotas()
    at, valid = [], []
    for face in range(6):
        near = nbr[block, face]
        valid.append(jnp.full((8, 128), near, jnp.int32) >= 0)
        at.append(jnp.clip(near - first, 0, 11))
    place = (lane // 16 - row % 2) % 8
    upper, lower = slice(X_SENT, X_SENT + 8), slice(X_SENT + 8, X_SENT + 16)
    out[slot, upper, :] = jnp.where(valid[1], packets[at[1], upper, :], -1.0)
    second = jnp.where(valid[1], packets[at[1], lower, :], -1.0)
    out[slot, lower, :] = jnp.where(row < 2, second, jnp.where(valid[0], packets[at[0], lower, :], -1.0))
    for v in range(3):
        rows = slice(Y_SENT + 8 * v, Y_SENT + 8 * v + 8)
        even_rows = jnp.where(valid[2], packets[at[2], rows, :], -1.0)
        odd_rows = jnp.where(valid[3], packets[at[3], rows, :], -1.0)
        value = jnp.where(row % 2 == 0, even_rows, odd_rows)
        if v > 0:
            value = jnp.where(place >= (7 if v == 1 else 5), jnp.where(valid[0], packets[at[0], rows, :], -1.0), value)
        out[slot, rows, :] = value
        rows = slice(Z_SENT + 8 * v, Z_SENT + 8 * v + 8)
        low = jnp.where(valid[4], packets[at[4], rows, :], -1.0)
        high = jnp.where(valid[5], packets[at[5], rows, :], -1.0)
        out[slot, rows, :] = jnp.where(lane % 2 == 0, low, high)


def outside(which, v):
    row, lane = grid_iotas()
    cx, cy, cz = VELOCITY[which]
    x_mask = y_mask = z_mask = None
    if cx == 1 and v == 0:
        x_mask = row < 2
    if cx == -1 and v == 3:
        x_mask = row >= 6
    if cy == 1:
        y_mask = (row % 2 == 0) & (lane < 16)
    if cy == -1:
        y_mask = (row % 2 == 1) & (lane >= 112)
    if cz == 1:
        z_mask = lane % 16 == 0
    if cz == -1:
        z_mask = lane % 16 == 15
    return x_mask, y_mask, z_mask


def build_halo(planes, halo):
    row, lane = grid_iotas()
    for which in range(1, 19):
        cx, cy, cz = VELOCITY[which]
        for v in range(4):
            x_mask, y_mask, z_mask = outside(which, v)
            value = None
            if z_mask is not None:
                face = 4 if cz == 1 else 5
                k = LEAVING[face ^ 1].index(which)
                by = 16 * cy - (2 * k + 1) + (-15 if cz == 1 else 15)
                start = Z_ROW + 8 * v - 2 * cx
                value = planes[start : start + 8, :]
                if cy != 0:
                    beside = planes[start - cy : start - cy + 8, :]
                    to = (lane + by) % 128
                    value = jnp.where(to < 16 if cy == 1 else to >= 112, beside, value)
                value = turned(value, by)
            if y_mask is not None:
                face = 2 if cy == 1 else 3
                k = LEAVING[face ^ 1].index(which)
                by = -16 * k if cy == 1 else 112 - 16 * (k + 1)
                start = Y_ROW + 8 * v - 2 * cx
                plane = planes[start : start + 8, :]
                line = turned(plane, by)
                if cz != 0:
                    line = jnp.where(lane % 16 == (0 if cz == 1 else 15), line, turned(plane, by + cz))
                value = line if value is None else jnp.where(y_mask, line, value)
            if x_mask is not None:
                face = 0 if cx == 1 else 1
                k = LEAVING[face ^ 1].index(which)
                at = X_ROW + 10 * (face ^ 1) + 2 * k
                pair = planes[at : at + 2, :]
                upper, lower = pair[0:1], pair[1:2]
                if cy == 1:
                    high, low = turned(upper, 16), turned(lower, 16)
                    lane1 = lane[0:1]
                    lower = jnp.where(lane1 < 16, high, low)
                    upper = jnp.where(lane1 < 16, upper, high)
                elif cy == -1:
                    high, low = turned(upper, -16), turned(lower, -16)
                    lane1 = lane[0:1]
                    upper = jnp.where(lane1 >= 112, low, high)
                    lower = jnp.where(lane1 >= 112, lower, low)
                elif cz != 0:
                    edge = lane[0:1] % 16 == (0 if cz == 1 else 15)
                    upper = jnp.where(edge, upper, turned(upper, cz))
                    lower = jnp.where(edge, lower, turned(lower, cz))
                both = jnp.where(
                    row % 2 == 0,
                    jnp.broadcast_to(upper, (8, 128)),
                    jnp.broadcast_to(lower, (8, 128)),
                )
                value = both if value is None else jnp.where(x_mask, both, value)
            if value is not None:
                halo[which, 8 * v : 8 * v + 8, :] = value


def collide(f, shear):
    s = {q: f[q] + f[q + 1] for q in range(1, 19, 2)}
    d = {q: f[q] - f[q + 1] for q in range(1, 19, 2)}
    sx, sy, sz = s[1], s[3], s[5]
    sxy, sxz, syz = s[7] + s[9], s[11] + s[13], s[15] + s[17]
    along = sx + (sy + sz)
    across = sxy + (sxz + syz)
    xa, xb = d[7] + d[9], d[11] + d[13]
    ya, yb = d[15] + d[17], d[7] - d[9]
    za, zb = d[11] - d[13], d[15] - d[17]
    x_sum, y_sum, z_sum = xa + xb, ya + yb, za + zb
    jx, jy, jz = d[1] + x_sum, d[3] + y_sum, d[5] + z_sum
    xx, yy, zz = jx * jx, jy * jy, jz * jz
    yz_sum = yy + zz
    jj = xx + yz_sum
    e1 = (1.19 * 19.0 / 2394.0) * ((across - f[0]) - jj)
    e2 = (1.4 / 252.0) * ((9.0 * f[0] - 7.0 * along) - (2.0 * across - 5.5 * jj))
    qx = (1.2 / 40.0 * 5.0 / 3.0) * (x_sum - 2.0 * d[1])
    qy = (1.2 / 40.0 * 5.0 / 3.0) * (y_sum - 2.0 * d[3])
    qz = (1.2 / 40.0 * 5.0 / 3.0) * (z_sum - 2.0 * d[5])
    axial = (2.0 * sx) - (sy + sz)
    planar = (sxy + sxz) - 2.0 * syz
    stress = 2.0 * xx - yz_sum
    e9 = (shear * (1.0 / 36.0)) * ((axial + planar) - stress)
    e10 = (1.4 / 72.0) * ((planar - 2.0 * axial) + 0.5 * stress)
    axial_w = sy - sz
    planar_w = sxy - sxz
    stress_w = yy - zz
    e11 = (shear * (1.0 / 12.0)) * ((axial_w + planar_w) - stress_w)
    e12 = (1.4 / 24.0) * ((planar_w - 2.0 * axial_w) + 0.5 * stress_w)
    quarter = shear * 0.25
    e13 = quarter * ((s[7] - s[9]) - jx * jy)
    e14 = quarter * ((s[15] - s[17]) - jy * jz)
    e15 = quarter * ((s[11] - s[13]) - jx * jz)
    e16 = (1.98 / 8.0) * (xa - xb)
    e17 = (1.98 / 8.0) * (ya - yb)
    e18 = (1.98 / 8.0) * (za - zb)
    post = [None] * 19
    post[0] = f[0] + (30.0 * e1 - 12.0 * e2)
    base = 11.0 * e1 + 4.0 * e2
    t9 = e9 - 2.0 * e10
    t11 = e11 - 2.0 * e12
    evens = {1: 2.0 * t9 - base, 3: t11 - (t9 + base), 5: -((t11 + t9) + base)}
    base = 8.0 * e1 + e2
    u9 = e9 + e10
    u11 = e11 + e12
    upper, lower, third = base + u9 + u11, base + u9 - u11, base - 2.0 * u9
    evens.update({7: upper + e13, 9: upper - e13, 11: lower + e15, 13: lower - e15, 15: third + e14, 17: third - e14})
    xp, xm = qx + e16, qx - e16
    yp, ym = qy + e17, qy - e17
    zp, zm = qz + e18, qz - e18
    odds = {
        1: -4.0 * qx, 3: -4.0 * qy, 5: -4.0 * qz,
        7: xp + ym, 9: xp - ym, 11: xm + zp, 13: xm - zp, 15: yp + zm, 17: yp - zm,
    }
    for q in range(1, 19, 2):
        post[q] = f[q] - (evens[q] + odds[q])
        post[q + 1] = f[q + 1] - (evens[q] - odds[q])
    return post


def arrived(q, v, post, halo):
    _, lane = grid_iotas()
    cx, cy, cz = VELOCITY[q]
    start = TOP + 8 * v - 2 * cx
    value = post[q, start : start + 8, :]
    by = 16 * cy + cz
    if cy != 0:
        beside = post[q, start - cy : start - cy + 8, :]
        value = jnp.where(lane >= 128 - by if cy == 1 else lane < -by, beside, value)
    value = turned(value, by)
    masks = [m for m in outside(q, v) if m is not None]
    if masks:
        edge = halo[q, 8 * v : 8 * v + 8, :]
        bounced = post[OPPOSITE[q], TOP + 8 * v : TOP + 8 * v + 8, :]
        value = jnp.where(functools.reduce(jnp.logical_or, masks), jnp.where(edge < 0.0, bounced, edge), value)
    return value


def collide_first(first, post, shear):
    for v in range(4):
        values = collide([first[q, 8 * v : 8 * v + 8, :] for q in range(19)], shear)
        for q in range(19):
            post[q, TOP + 8 * v : TOP + 8 * v + 8, :] = values[q]


def run_and_collide(state, post, target, halo, shear):
    for v in range(4):
        values = [arrived(q, v, post, halo) for q in range(19)]
        for q in range(19):
            state[q, 8 * v : 8 * v + 8, :] = values[q]
        values = collide(values, shear)
        for q in range(19):
            target[q, TOP + 8 * v : TOP + 8 * v + 8, :] = values[q]


def run_last(state, post, halo):
    for v in range(4):
        for q in range(19):
            state[q, 8 * v : 8 * v + 8, :] = arrived(q, v, post, halo)


def kernel(
    sizes, pop, nbr_in, sub_in, moves_in, out, ids, raw, nbr, sub, moves, mine, theirs, state, cube, packets, gone, interface_out, first, interface, planes, corner, post, halo,
    load_sem, send_sem, recv_sem, answer_sem, near_sem, across_sem,
):
    ny, nz, total = sizes
    bit = ny * nz
    me = lax.axis_index("gx") * bit + lax.axis_index("gy") * nz + lax.axis_index("gz")

    def place(d):
        return (d // bit, d // nz % ny, d % nz)

    partner_id = lax.rem(me // bit, 2) * (-2 * bit) + bit + me
    partner = place(partner_id)
    later = place(lax.rem(me + 1, total))
    before = place(lax.rem(me + total - 1, total))

    loads = [
        pltpu.make_async_copy(source, target, load_sem.at[k]) for k, (source, target) in enumerate(((pop, raw), (nbr_in, nbr), (sub_in, sub), (moves_in, moves)))
    ]
    for load in loads:
        load.start()

    odd = lax.rem(me // bit, 2) == 1
    inner = lax.rem(me, bit)
    at_start, at_end = inner == 0, inner == bit - 1
    even = jnp.logical_not(odd)
    barrier = pltpu.get_barrier_semaphore()

    def signal(semaphore, device):
        pl.semaphore_signal(semaphore, inc=1, device_id=device, device_id_type=MESH)

    @pl.when(odd)
    def _():
        signal(barrier, partner)

    @pl.when(even & at_start)
    def _():
        signal(barrier, before)

    @pl.when(odd & at_start)
    def _():
        signal(barrier, before)

    def remote(source, target, number, device):
        return pltpu.make_async_remote_copy(
            src_ref=source,
            dst_ref=target,
            send_sem=send_sem.at[number],
            recv_sem=recv_sem.at[number],
            device_id=device,
            device_id_type=MESH,
        )

    @pl.when(even & jnp.logical_not(at_end))
    def _():
        pl.semaphore_wait(barrier, 1)

    @pl.when(even & at_end)
    def _():
        pl.semaphore_wait(barrier, 2)
        signal(across_sem, later)

    @pl.when(even)
    def _():
        signal(answer_sem, partner)

    @pl.when(odd)
    def _():
        pl.semaphore_wait(answer_sem, 1)

    @pl.when(odd & jnp.logical_not(at_start))
    def _():
        signal(barrier, before)

    @pl.when(odd & jnp.logical_not(at_end))
    def _():
        signal(barrier, later)

    gz = lax.rem(me, nz)
    z_low = lax.rem(me // nz, ny) // 2
    lowest_chips = z_low < ny // 4
    late = gz >= nz // 2

    def hear():
        @pl.when(odd & jnp.logical_not(at_start))
        def _():
            pl.semaphore_wait(barrier, 2)

        @pl.when(odd & at_start)
        def _():
            pl.semaphore_wait(barrier, 1)

        @pl.when(odd)
        def _():
            signal(near_sem, partner)

        @pl.when(odd & at_end)
        def _():
            signal(across_sem, later)


    for load in loads:
        load.wait()

    moved = [moves[0, 0], moves[0, 1]]
    for k in range(4):
        mine[0, k] = sub[k]
        mine[1, k] = moves[0, k % 2]
    orders = remote(mine, theirs, 12, partner)
    orders.start()
    blocks = [remote(gone.at[k], first.at[2 + k], k, partner) for k in range(2)]
    for k in range(2):
        for q in range(19):
            for v in range(4):
                gone[k, q, 8 * v : 8 * v + 8, :] = raw[q, pl.ds(32 * v + moved[k], 8, stride=4), :]
        blocks[k].start()

    for b in range(4):
        unpacked(raw, cube, b)

    hear()

    pack_faces(cube, packets, 0, 4, corner)

    @pl.when(even)
    def _():
        pl.semaphore_wait(near_sem, 1)

    @pl.when(at_start)
    def _():
        pl.semaphore_wait(across_sem, 1)

    far_later = (gz == nz // 2 - 1) | (gz == nz - 1)
    far_before = (gz == nz // 2) | (gz == 0)
    early = (far_later | far_before) & jnp.logical_not(late) & lowest_chips
    urgent = lowest_chips | at_end | jnp.logical_not(late)
    halos = []
    for b in range(4):
        if b > 0:
            pack_faces(cube, packets, b, 4 + b, corner)
        for number, at, device, far in ((4 + b, b, later, far_later), (8 + b, 8 + b, before, far_before)):
            copy = remote(packets.at[4 + b], packets.at[at], number, device)
            pl.when(far & urgent)(copy.start)
            halos.append((copy, far))
    for copy, far in halos:
        pl.when(jnp.logical_not(far))(copy.start)

    low = jnp.minimum(moved[0], moved[1])
    high = jnp.maximum(moved[0], moved[1])
    stay0 = jnp.where(low > 0, 0, jnp.where(high > 1, 1, 2))
    stay1 = jnp.minimum(6 - low - high - stay0, 3)

    def keep(j, carry):
        stay = jnp.where(j == 0, stay0, stay1)

        def one(q, inner_carry):
            first[j, q] = cube[stay, q, TOP : TOP + 32, :]
            return inner_carry

        lax.fori_loop(0, 19, one, 0)
        count = jnp.full((8, 128), sub[stay], jnp.int32).astype(jnp.float32)
        collide_first(first.at[j], post.at[j, 0], 1.0 / (count * (1.0 / 1.6 - 0.5) + 0.5))
        return carry

    lax.fori_loop(0, 2, keep, 0)

    for copy, far in halos:
        pl.when(far & jnp.logical_not(urgent))(copy.start)

    orders.wait_recv()

    def shear_of(j):
        came = theirs[0, jnp.clip(theirs[1, jnp.clip(j - 2, 0, 1)], 0, 3)]
        count = jnp.where(j == 0, sub[stay0], jnp.where(j == 1, sub[stay1], came))
        return 1.0 / (jnp.full((8, 128), count, jnp.int32).astype(jnp.float32) * (1.0 / 1.6 - 0.5) + 0.5)

    def start_foreign():
        for copy in blocks:
            copy.wait_recv()

        def one(j, carry):
            collide_first(first.at[j], post.at[j, 0], shear_of(j))
            return carry

        lax.fori_loop(2, 4, one, 0)

    pl.when(early)(start_foreign)

    for copy, _ in halos:
        copy.wait_recv()

    lowest = (me - 1) * 4
    faces = []
    for k in range(2):
        assemble(packets, nbr, moved[k], lowest, interface_out, k)
        copy = remote(interface_out.at[k], interface.at[2 + k], 2 + k, partner)
        copy.start()
        faces.append(copy)

    for j, stay in enumerate((stay0, stay1)):
        assemble(packets, nbr, stay, lowest, interface, j)

    def job(j, carry):
        for k in range(2):
            @pl.when(j == 2 + k)
            def _(k=k):
                faces[k].wait_recv()

        pl.when((j == 2) & jnp.logical_not(early))(start_foreign)
        shear = shear_of(j)
        spread(interface, j, planes)
        build_halo(planes, halo)

        def one(step, inner_carry):
            now = lax.rem(step, 2)
            run_and_collide(state.at[step, j], post.at[j, now], post.at[j, 1 - now], halo, shear)
            return inner_carry

        lax.fori_loop(0, 3, one, 0)
        run_last(state.at[3, j], post.at[j, 1], halo)
        return carry

    lax.fori_loop(0, 4, job, 0)

    for s in range(4):
        here = jnp.where(moved[0] == s, 2, jnp.where(moved[1] == s, 3, jnp.where(stay0 == s, 0, 1)))
        sent = jnp.where(moved[0] == s, theirs[1, 0], theirs[1, 1])
        foreign = here >= 2
        count = jnp.where(foreign, theirs[0, jnp.clip(sent, 0, 3)], sub[s])
        step = jnp.clip(count - 1, 0, 3)
        for q in range(19):
            for v in range(4):
                out[q, pl.ds(32 * v + s, 8, stride=4), :] = state[step, here, q, 8 * v : 8 * v + 8, :]
        ids[s] = jnp.where(foreign, partner_id * 4 + sent, me * 4 + s)

    for copy in [copy for copy, _ in halos] + blocks + faces + [orders]:
        copy.wait_send()


def write(result, ids_in, out, ids, sems):
    copies = [pltpu.make_async_copy(ids_in, ids, sems.at[4])]
    for k, (low, count) in enumerate(((0, 5), (5, 5), (10, 5), (15, 4))):
        part = pl.ds(low, count)
        copies.append(pltpu.make_async_copy(result.at[part], out.at[part], sems.at[k]))
    for copy in copies:
        copy.start()
    for copy in copies:
        copy.wait()


def shards(sizes, populations, neighbours, substeps, moves):
    f32 = jnp.float32
    lying = populations.reshape(4, 19, 32, 128).transpose(1, 2, 0, 3).reshape(19, 128, 128)
    vmem, smem = pl.BlockSpec(memory_space=pltpu.VMEM), pl.BlockSpec(memory_space=pltpu.SMEM)
    whole = pl.BlockSpec(memory_space=pl.ANY)
    shapes = (jax.ShapeDtypeStruct((19, 128, 128), f32), jax.ShapeDtypeStruct((4,), jnp.int32))
    result, ids = pl.pallas_call(
        functools.partial(kernel, sizes),
        out_shape=(pltpu.VMEM((19, 128, 128), f32), shapes[1]),
        in_specs=[pl.BlockSpec(memory_space=pltpu.HBM)] * 4,
        out_specs=(vmem, smem),
        scratch_shapes=[
            pltpu.VMEM((19, 128, 128), f32),
            pltpu.SMEM((4, 6), jnp.int32),
            pltpu.SMEM((4,), jnp.int32),
            pltpu.SMEM((1, 2), jnp.int32),
            pltpu.SMEM((2, 4), jnp.int32),
            pltpu.SMEM((2, 4), jnp.int32),
            pltpu.VMEM((4, 4, 19, 32, 128), f32),
            pltpu.VMEM((4, 19, 48, 128), f32),
            pltpu.VMEM((12, SENT_ROWS, 128), f32),
            pltpu.VMEM((2, 19, 32, 128), f32),
            pltpu.VMEM((2, SENT_ROWS, 128), f32),
            pltpu.VMEM((4, 19, 32, 128), f32),
            pltpu.VMEM((4, SENT_ROWS, 128), f32),
            pltpu.VMEM((PLANE_ROWS, 128), f32),
            pltpu.VMEM((8, 128), f32),
            pltpu.VMEM((4, 2, 19, 48, 128), f32),
            pltpu.VMEM((19, 32, 128), f32),
            pltpu.SemaphoreType.DMA((4,)),
            pltpu.SemaphoreType.DMA((13,)),
            pltpu.SemaphoreType.DMA((13,)),
            pltpu.SemaphoreType.REGULAR,
            pltpu.SemaphoreType.REGULAR,
            pltpu.SemaphoreType.REGULAR,
        ],
        compiler_params=pltpu.CompilerParams(
            collective_id=0, has_side_effects=True, vmem_limit_bytes=53500 * 1024
        ),
        name="lattice_step",
    )(*[pltpu.with_memory_space_constraint(value, pltpu.HBM) for value in (lying, neighbours, substeps, moves)])
    result, ids = pl.pallas_call(
        write,
        out_shape=shapes,
        in_specs=[vmem, whole],
        out_specs=(whole, whole),
        scratch_shapes=[pltpu.SemaphoreType.DMA((5,))],
        compiler_params=pltpu.CompilerParams(vmem_limit_bytes=36 * 1024 * 1024),
        name="write_out",
    )(result, ids)
    return result.reshape(19, 32, 4, 128).transpose(2, 0, 1, 3).reshape(4, 19, 4096), ids


def solution(mesh):
    sizes = (mesh.shape["gy"], mesh.shape["gz"], mesh.size)
    return jax.shard_map(
        functools.partial(shards, sizes),
        mesh=mesh,
        in_specs=(P(AXES, None, None), P(AXES, None), P(AXES), P(AXES, None)),
        out_specs=(P(AXES, None, None), P(AXES)),
        check_vma=False,
    )
```

```python
import functools

import jax
import jax.numpy as jnp
import numpy as np
from jax import lax
from jax.experimental import pallas as pl
from jax.experimental.pallas import tpu as pltpu
from jax.sharding import PartitionSpec as P

MESH = pl.DeviceIdType.MESH
AXES = ("gx", "gy", "gz")
VELOCITY = [
    (0, 0, 0), (1, 0, 0), (-1, 0, 0), (0, 1, 0), (0, -1, 0), (0, 0, 1), (0, 0, -1),
    (1, 1, 0), (-1, -1, 0), (1, -1, 0), (-1, 1, 0), (1, 0, 1), (-1, 0, -1),
    (1, 0, -1), (-1, 0, 1), (0, 1, 1), (0, -1, -1), (0, 1, -1), (0, -1, 1),
]
OPPOSITE = [0, 2, 1, 4, 3, 6, 5, 8, 7, 10, 9, 12, 11, 14, 13, 16, 15, 18, 17]
LEAVING = [
    [2, 8, 10, 12, 14], [1, 7, 9, 11, 13], [4, 8, 9, 16, 18],
    [3, 7, 10, 15, 17], [6, 12, 13, 16, 17], [5, 11, 14, 15, 18],
]
Y_SENT, Z_SENT, X_SENT, SENT_ROWS = 0, 24, 48, 64
X_ROW, Y_ROW, Z_ROW, PLANE_ROWS = 0, 24, 56, 96
TOP = 8


def turned(value, by):
    by = by % 128
    return value if by == 0 else pltpu.roll(value, by, 1)


def grid_iotas():
    row = lax.broadcasted_iota(jnp.int32, (8, 128), 0)
    lane = lax.broadcasted_iota(jnp.int32, (8, 128), 1)
    return row, lane


def unpacked(raw, cube, block):
    for q in range(19):
        for v in range(4):
            cube[block, q, TOP + 8 * v : TOP + 8 * v + 8, :] = raw[q, pl.ds(32 * v + block, 8, stride=4), :]


def pack_faces(cube, packets, block, slot, corner):
    row, lane = grid_iotas()
    even = row % 2 == 0
    place = (lane // 16 - row % 2) % 8
    for face in range(2):
        start = TOP if face == 0 else TOP + 30
        for k in range(5):
            at = 10 * face + 2 * k
            pair = cube[block, LEAVING[face][k], start : start + 2, :]
            if at < 16:
                packets[slot, X_SENT + at : X_SENT + at + 2, :] = pair
            else:
                corner[at - 16 : at - 14, :] = pair
                corner[at - 12 : at - 10, :] = pair
    ys, zs = [], []
    for v in range(4):
        base = TOP + 8 * v
        kept = jnp.zeros((8, 128), jnp.float32)
        for k in range(5):
            far = cube[block, LEAVING[3][k], base + 1 : base + 9, :]
            near = cube[block, LEAVING[2][k], base - 1 : base + 7, :]
            moved = turned(jnp.where(even, far, near), 16 * (k + 1))
            kept = jnp.where(place == k, moved, kept)
        ys.append(kept)
        kept = jnp.zeros((8, 128), jnp.float32)
        for k in range(5):
            near = cube[block, LEAVING[4][k], base : base + 8, :]
            far = cube[block, LEAVING[5][k], base : base + 8, :]
            moved = turned(jnp.where(lane % 16 == 15, far, near), 2 * k + 1)
            kept = jnp.where(lane % 16 // 2 == k, moved, kept)
        zs.append(kept)
    ys[0] = jnp.where(place >= 5, turned(ys[3], 80), ys[0])
    ys[1] = jnp.where(place >= 5, turned(ys[3], 32), ys[1])
    zs[0] = jnp.where(lane % 16 >= 10, turned(zs[3], 10), zs[0])
    zs[1] = jnp.where(lane % 16 >= 10, turned(zs[3], 4), zs[1])
    rest = corner[...]
    rest = jnp.where(row < 4, rest, turned(rest, 64))
    ys[1] = jnp.where(place == 7, jnp.where(even, turned(rest, 64), turned(rest, 80)), ys[1])
    ys[2] = jnp.where(place >= 5, jnp.where(even, turned(rest, 80), turned(rest, 96)), ys[2])
    for v in range(3):
        packets[slot, Y_SENT + 8 * v : Y_SENT + 8 * v + 8, :] = ys[v]
        packets[slot, Z_SENT + 8 * v : Z_SENT + 8 * v + 8, :] = zs[v]


def spread(sent, slot, planes):
    row, lane = grid_iotas()
    place = (lane // 16 - row % 2) % 8
    ys = [sent[slot, Y_SENT + 8 * v : Y_SENT + 8 * v + 8, :] for v in range(3)]
    zs = [sent[slot, Z_SENT + 8 * v : Z_SENT + 8 * v + 8, :] for v in range(3)]
    ys.append(jnp.where(place < 3, turned(ys[0], -80), turned(ys[1], -32)))
    zs.append(jnp.where(lane % 16 < 6, turned(zs[0], -10), turned(zs[1], -4)))
    for v in range(4):
        planes[Y_ROW + 8 * v : Y_ROW + 8 * v + 8, :] = ys[v]
        planes[Z_ROW + 8 * v : Z_ROW + 8 * v + 8, :] = zs[v]
    for v in range(2):
        planes[X_ROW + 8 * v : X_ROW + 8 * v + 8, :] = sent[slot, X_SENT + 8 * v : X_SENT + 8 * v + 8, :]
    even = row % 2 == 0
    one = jnp.where(even, turned(ys[1], -64), turned(ys[1], -80))
    rest = jnp.where(lane // 16 == 3, one, jnp.where(even, turned(ys[2], -80), turned(ys[2], -96)))
    planes[X_ROW + 16 : X_ROW + 24, :] = rest
    below = turned(planes[X_ROW + 20 : X_ROW + 28, :], 64)
    planes[X_ROW + 16 : X_ROW + 20, :] = jnp.where(lane < 64, rest, below)[0:4]


def assemble(packets, nbr, block, first, out, slot):
    row, lane = grid_iotas()
    at, valid = [], []
    for face in range(6):
        near = nbr[block, face]
        valid.append(jnp.full((8, 128), near, jnp.int32) >= 0)
        at.append(jnp.clip(near - first, 0, 11))
    place = (lane // 16 - row % 2) % 8
    upper, lower = slice(X_SENT, X_SENT + 8), slice(X_SENT + 8, X_SENT + 16)
    out[slot, upper, :] = jnp.where(valid[1], packets[at[1], upper, :], -1.0)
    second = jnp.where(valid[1], packets[at[1], lower, :], -1.0)
    out[slot, lower, :] = jnp.where(row < 2, second, jnp.where(valid[0], packets[at[0], lower, :], -1.0))
    for v in range(3):
        rows = slice(Y_SENT + 8 * v, Y_SENT + 8 * v + 8)
        even_rows = jnp.where(valid[2], packets[at[2], rows, :], -1.0)
        odd_rows = jnp.where(valid[3], packets[at[3], rows, :], -1.0)
        value = jnp.where(row % 2 == 0, even_rows, odd_rows)
        if v > 0:
            value = jnp.where(place >= (7 if v == 1 else 5), jnp.where(valid[0], packets[at[0], rows, :], -1.0), value)
        out[slot, rows, :] = value
        rows = slice(Z_SENT + 8 * v, Z_SENT + 8 * v + 8)
        low = jnp.where(valid[4], packets[at[4], rows, :], -1.0)
        high = jnp.where(valid[5], packets[at[5], rows, :], -1.0)
        out[slot, rows, :] = jnp.where(lane % 2 == 0, low, high)


def outside(which, v):
    row, lane = grid_iotas()
    cx, cy, cz = VELOCITY[which]
    x_mask = y_mask = z_mask = None
    if cx == 1 and v == 0:
        x_mask = row < 2
    if cx == -1 and v == 3:
        x_mask = row >= 6
    if cy == 1:
        y_mask = (row % 2 == 0) & (lane < 16)
    if cy == -1:
        y_mask = (row % 2 == 1) & (lane >= 112)
    if cz == 1:
        z_mask = lane % 16 == 0
    if cz == -1:
        z_mask = lane % 16 == 15
    return x_mask, y_mask, z_mask


def build_halo(planes, halo):
    row, lane = grid_iotas()
    for which in range(1, 19):
        cx, cy, cz = VELOCITY[which]
        for v in range(4):
            x_mask, y_mask, z_mask = outside(which, v)
            value = None
            if z_mask is not None:
                face = 4 if cz == 1 else 5
                k = LEAVING[face ^ 1].index(which)
                by = 16 * cy - (2 * k + 1) + (-15 if cz == 1 else 15)
                start = Z_ROW + 8 * v - 2 * cx
                value = planes[start : start + 8, :]
                if cy != 0:
                    beside = planes[start - cy : start - cy + 8, :]
                    to = (lane + by) % 128
                    value = jnp.where(to < 16 if cy == 1 else to >= 112, beside, value)
                value = turned(value, by)
            if y_mask is not None:
                face = 2 if cy == 1 else 3
                k = LEAVING[face ^ 1].index(which)
                by = -16 * k if cy == 1 else 112 - 16 * (k + 1)
                start = Y_ROW + 8 * v - 2 * cx
                plane = planes[start : start + 8, :]
                line = turned(plane, by)
                if cz != 0:
                    line = jnp.where(lane % 16 == (0 if cz == 1 else 15), line, turned(plane, by + cz))
                value = line if value is None else jnp.where(y_mask, line, value)
            if x_mask is not None:
                face = 0 if cx == 1 else 1
                k = LEAVING[face ^ 1].index(which)
                at = X_ROW + 10 * (face ^ 1) + 2 * k
                pair = planes[at : at + 2, :]
                upper, lower = pair[0:1], pair[1:2]
                if cy == 1:
                    high, low = turned(upper, 16), turned(lower, 16)
                    lane1 = lane[0:1]
                    lower = jnp.where(lane1 < 16, high, low)
                    upper = jnp.where(lane1 < 16, upper, high)
                elif cy == -1:
                    high, low = turned(upper, -16), turned(lower, -16)
                    lane1 = lane[0:1]
                    upper = jnp.where(lane1 >= 112, low, high)
                    lower = jnp.where(lane1 >= 112, lower, low)
                elif cz != 0:
                    edge = lane[0:1] % 16 == (0 if cz == 1 else 15)
                    upper = jnp.where(edge, upper, turned(upper, cz))
                    lower = jnp.where(edge, lower, turned(lower, cz))
                both = jnp.where(
                    row % 2 == 0,
                    jnp.broadcast_to(upper, (8, 128)),
                    jnp.broadcast_to(lower, (8, 128)),
                )
                value = both if value is None else jnp.where(x_mask, both, value)
            if value is not None:
                halo[which, 8 * v : 8 * v + 8, :] = value


def collide(f, shear):
    s = {q: f[q] + f[q + 1] for q in range(1, 19, 2)}
    d = {q: f[q] - f[q + 1] for q in range(1, 19, 2)}
    sx, sy, sz = s[1], s[3], s[5]
    sxy, sxz, syz = s[7] + s[9], s[11] + s[13], s[15] + s[17]
    along = sx + (sy + sz)
    across = sxy + (sxz + syz)
    xa, xb = d[7] + d[9], d[11] + d[13]
    ya, yb = d[15] + d[17], d[7] - d[9]
    za, zb = d[11] - d[13], d[15] - d[17]
    x_sum, y_sum, z_sum = xa + xb, ya + yb, za + zb
    jx, jy, jz = d[1] + x_sum, d[3] + y_sum, d[5] + z_sum
    xx, yy, zz = jx * jx, jy * jy, jz * jz
    yz_sum = yy + zz
    jj = xx + yz_sum
    e1 = (1.19 * 19.0 / 2394.0) * ((across - f[0]) - jj)
    e2 = (1.4 / 252.0) * ((9.0 * f[0] - 7.0 * along) - (2.0 * across - 5.5 * jj))
    qx = (1.2 / 40.0 * 5.0 / 3.0) * (x_sum - 2.0 * d[1])
    qy = (1.2 / 40.0 * 5.0 / 3.0) * (y_sum - 2.0 * d[3])
    qz = (1.2 / 40.0 * 5.0 / 3.0) * (z_sum - 2.0 * d[5])
    axial = (2.0 * sx) - (sy + sz)
    planar = (sxy + sxz) - 2.0 * syz
    stress = 2.0 * xx - yz_sum
    e9 = (shear * (1.0 / 36.0)) * ((axial + planar) - stress)
    e10 = (1.4 / 72.0) * ((planar - 2.0 * axial) + 0.5 * stress)
    axial_w = sy - sz
    planar_w = sxy - sxz
    stress_w = yy - zz
    e11 = (shear * (1.0 / 12.0)) * ((axial_w + planar_w) - stress_w)
    e12 = (1.4 / 24.0) * ((planar_w - 2.0 * axial_w) + 0.5 * stress_w)
    quarter = shear * 0.25
    e13 = quarter * ((s[7] - s[9]) - jx * jy)
    e14 = quarter * ((s[15] - s[17]) - jy * jz)
    e15 = quarter * ((s[11] - s[13]) - jx * jz)
    e16 = (1.98 / 8.0) * (xa - xb)
    e17 = (1.98 / 8.0) * (ya - yb)
    e18 = (1.98 / 8.0) * (za - zb)
    post = [None] * 19
    post[0] = f[0] + (30.0 * e1 - 12.0 * e2)
    base = 11.0 * e1 + 4.0 * e2
    t9 = e9 - 2.0 * e10
    t11 = e11 - 2.0 * e12
    evens = {1: 2.0 * t9 - base, 3: t11 - (t9 + base), 5: -((t11 + t9) + base)}
    base = 8.0 * e1 + e2
    u9 = e9 + e10
    u11 = e11 + e12
    upper, lower, third = base + u9 + u11, base + u9 - u11, base - 2.0 * u9
    evens.update({7: upper + e13, 9: upper - e13, 11: lower + e15, 13: lower - e15, 15: third + e14, 17: third - e14})
    xp, xm = qx + e16, qx - e16
    yp, ym = qy + e17, qy - e17
    zp, zm = qz + e18, qz - e18
    odds = {
        1: -4.0 * qx, 3: -4.0 * qy, 5: -4.0 * qz,
        7: xp + ym, 9: xp - ym, 11: xm + zp, 13: xm - zp, 15: yp + zm, 17: yp - zm,
    }
    for q in range(1, 19, 2):
        post[q] = f[q] - (evens[q] + odds[q])
        post[q + 1] = f[q + 1] - (evens[q] - odds[q])
    return post


def arrived(q, v, post, halo):
    _, lane = grid_iotas()
    cx, cy, cz = VELOCITY[q]
    start = TOP + 8 * v - 2 * cx
    value = post[q, start : start + 8, :]
    by = 16 * cy + cz
    if cy != 0:
        beside = post[q, start - cy : start - cy + 8, :]
        value = jnp.where(lane >= 128 - by if cy == 1 else lane < -by, beside, value)
    value = turned(value, by)
    masks = [m for m in outside(q, v) if m is not None]
    if masks:
        edge = halo[q, 8 * v : 8 * v + 8, :]
        bounced = post[OPPOSITE[q], TOP + 8 * v : TOP + 8 * v + 8, :]
        value = jnp.where(functools.reduce(jnp.logical_or, masks), jnp.where(edge < 0.0, bounced, edge), value)
    return value


def collide_first(first, post, shear):
    for v in range(4):
        values = collide([first[q, 8 * v : 8 * v + 8, :] for q in range(19)], shear)
        for q in range(19):
            post[q, TOP + 8 * v : TOP + 8 * v + 8, :] = values[q]


def run_and_collide(state, post, target, halo, shear):
    for v in range(4):
        values = [arrived(q, v, post, halo) for q in range(19)]
        for q in range(19):
            state[q, 8 * v : 8 * v + 8, :] = values[q]
        values = collide(values, shear)
        for q in range(19):
            target[q, TOP + 8 * v : TOP + 8 * v + 8, :] = values[q]


def run_last(state, post, halo):
    for v in range(4):
        for q in range(19):
            state[q, 8 * v : 8 * v + 8, :] = arrived(q, v, post, halo)


def kernel(
    sizes, pop, nbr_in, sub_in, moves_in, out, ids, raw, nbr, sub, moves, mine, theirs, state, cube, packets, gone, interface_out, first, interface, planes, corner, post, halo,
    load_sem, send_sem, recv_sem, answer_sem, near_sem, across_sem,
):
    ny, nz, total = sizes
    bit = ny * nz
    me = lax.axis_index("gx") * bit + lax.axis_index("gy") * nz + lax.axis_index("gz")

    def place(d):
        return (d // bit, d // nz % ny, d % nz)

    partner_id = lax.rem(me // bit, 2) * (-2 * bit) + bit + me
    partner = place(partner_id)
    later = place(lax.rem(me + 1, total))
    before = place(lax.rem(me + total - 1, total))

    loads = [
        pltpu.make_async_copy(source, target, load_sem.at[k]) for k, (source, target) in enumerate(((pop, raw), (nbr_in, nbr), (sub_in, sub), (moves_in, moves)))
    ]
    for load in loads:
        load.start()

    greeter = lax.rem(me // bit, 2) == 0
    inner = lax.rem(me, bit)
    at_start, at_end = inner == 0, inner == bit - 1
    answerer = jnp.logical_not(greeter)
    barrier = pltpu.get_barrier_semaphore()

    def signal(semaphore, device):
        pl.semaphore_signal(semaphore, inc=1, device_id=device, device_id_type=MESH)

    @pl.when(greeter)
    def _():
        signal(barrier, partner)

    @pl.when(answerer & at_start)
    def _():
        signal(barrier, before)

    @pl.when(greeter & at_start)
    def _():
        signal(barrier, before)

    def remote(source, target, number, device):
        return pltpu.make_async_remote_copy(
            src_ref=source,
            dst_ref=target,
            send_sem=send_sem.at[number],
            recv_sem=recv_sem.at[number],
            device_id=device,
            device_id_type=MESH,
        )

    @pl.when(answerer & jnp.logical_not(at_end))
    def _():
        pl.semaphore_wait(barrier, 1)

    @pl.when(answerer & at_end)
    def _():
        pl.semaphore_wait(barrier, 2)
        signal(across_sem, later)

    @pl.when(answerer)
    def _():
        signal(answer_sem, partner)

    @pl.when(greeter)
    def _():
        pl.semaphore_wait(answer_sem, 1)

    @pl.when(greeter & jnp.logical_not(at_start))
    def _():
        signal(barrier, before)

    @pl.when(greeter & jnp.logical_not(at_end))
    def _():
        signal(barrier, later)

    gz = lax.rem(me, nz)
    z_low = lax.rem(me // nz, ny) // 2
    lowest_chips = z_low < ny // 4
    late = gz >= nz // 2

    def hear():
        @pl.when(greeter & jnp.logical_not(at_start))
        def _():
            pl.semaphore_wait(barrier, 2)

        @pl.when(greeter & at_start)
        def _():
            pl.semaphore_wait(barrier, 1)

        @pl.when(greeter)
        def _():
            signal(near_sem, partner)

        @pl.when(greeter & at_end)
        def _():
            signal(across_sem, later)


    for load in loads:
        load.wait()

    moved = [moves[0, 0], moves[0, 1]]
    for k in range(4):
        mine[0, k] = sub[k]
        mine[1, k] = moves[0, k % 2]
    orders = remote(mine, theirs, 12, partner)
    orders.start()
    blocks = [remote(gone.at[k], first.at[2 + k], k, partner) for k in range(2)]
    for k in range(2):
        for q in range(19):
            for v in range(4):
                gone[k, q, 8 * v : 8 * v + 8, :] = raw[q, pl.ds(32 * v + moved[k], 8, stride=4), :]
        blocks[k].start()

    for b in range(4):
        unpacked(raw, cube, b)

    hear()

    pack_faces(cube, packets, 0, 4, corner)

    @pl.when(answerer)
    def _():
        pl.semaphore_wait(near_sem, 1)

    @pl.when(at_start)
    def _():
        pl.semaphore_wait(across_sem, 1)

    far_later = (gz == nz // 2 - 1) | (gz == nz - 1)
    far_before = (gz == nz // 2) | (gz == 0)
    early = (far_later | far_before) & jnp.logical_not(late) & lowest_chips
    urgent = lowest_chips | at_end | jnp.logical_not(late)
    halos = []
    for b in range(4):
        if b > 0:
            pack_faces(cube, packets, b, 4 + b, corner)
        for number, at, device, far in ((4 + b, b, later, far_later), (8 + b, 8 + b, before, far_before)):
            copy = remote(packets.at[4 + b], packets.at[at], number, device)
            pl.when(far & urgent)(copy.start)
            halos.append((copy, far))
    for copy, far in halos:
        pl.when(jnp.logical_not(far))(copy.start)

    low = jnp.minimum(moved[0], moved[1])
    high = jnp.maximum(moved[0], moved[1])
    stay0 = jnp.where(low > 0, 0, jnp.where(high > 1, 1, 2))
    stay1 = jnp.minimum(6 - low - high - stay0, 3)

    def keep(j, carry):
        stay = jnp.where(j == 0, stay0, stay1)

        def one(q, inner_carry):
            first[j, q] = cube[stay, q, TOP : TOP + 32, :]
            return inner_carry

        lax.fori_loop(0, 19, one, 0)
        count = jnp.full((8, 128), sub[stay], jnp.int32).astype(jnp.float32)
        collide_first(first.at[j], post.at[j, 0], 1.0 / (count * (1.0 / 1.6 - 0.5) + 0.5))
        return carry

    lax.fori_loop(0, 2, keep, 0)

    for copy, far in halos:
        pl.when(far & jnp.logical_not(urgent))(copy.start)

    orders.wait_recv()

    def shear_of(j):
        came = theirs[0, jnp.clip(theirs[1, jnp.clip(j - 2, 0, 1)], 0, 3)]
        count = jnp.where(j == 0, sub[stay0], jnp.where(j == 1, sub[stay1], came))
        return 1.0 / (jnp.full((8, 128), count, jnp.int32).astype(jnp.float32) * (1.0 / 1.6 - 0.5) + 0.5)

    def start_foreign():
        for copy in blocks:
            copy.wait_recv()

        def one(j, carry):
            collide_first(first.at[j], post.at[j, 0], shear_of(j))
            return carry

        lax.fori_loop(2, 4, one, 0)

    pl.when(early)(start_foreign)

    for copy, _ in halos:
        copy.wait_recv()

    lowest = (me - 1) * 4
    faces = []
    for k in range(2):
        assemble(packets, nbr, moved[k], lowest, interface_out, k)
        copy = remote(interface_out.at[k], interface.at[2 + k], 2 + k, partner)
        copy.start()
        faces.append(copy)

    for j, stay in enumerate((stay0, stay1)):
        assemble(packets, nbr, stay, lowest, interface, j)

    def job(j, carry):
        for k in range(2):
            @pl.when(j == 2 + k)
            def _(k=k):
                faces[k].wait_recv()

        pl.when((j == 2) & jnp.logical_not(early))(start_foreign)
        shear = shear_of(j)
        spread(interface, j, planes)
        build_halo(planes, halo)

        def one(step, inner_carry):
            now = lax.rem(step, 2)
            run_and_collide(state.at[step, j], post.at[j, now], post.at[j, 1 - now], halo, shear)
            return inner_carry

        lax.fori_loop(0, 3, one, 0)
        run_last(state.at[3, j], post.at[j, 1], halo)
        return carry

    lax.fori_loop(0, 4, job, 0)

    for s in range(4):
        here = jnp.where(moved[0] == s, 2, jnp.where(moved[1] == s, 3, jnp.where(stay0 == s, 0, 1)))
        sent = jnp.where(moved[0] == s, theirs[1, 0], theirs[1, 1])
        foreign = here >= 2
        count = jnp.where(foreign, theirs[0, jnp.clip(sent, 0, 3)], sub[s])
        step = jnp.clip(count - 1, 0, 3)
        for q in range(19):
            for v in range(4):
                out[q, pl.ds(32 * v + s, 8, stride=4), :] = state[step, here, q, 8 * v : 8 * v + 8, :]
        ids[s] = jnp.where(foreign, partner_id * 4 + sent, me * 4 + s)

    for copy in [copy for copy, _ in halos] + blocks + faces + [orders]:
        copy.wait_send()


def write(result, ids_in, out, ids, sems):
    copies = [pltpu.make_async_copy(ids_in, ids, sems.at[4])]
    for k, (low, count) in enumerate(((0, 5), (5, 5), (10, 5), (15, 4))):
        part = pl.ds(low, count)
        copies.append(pltpu.make_async_copy(result.at[part], out.at[part], sems.at[k]))
    for copy in copies:
        copy.start()
    for copy in copies:
        copy.wait()


def shards(sizes, populations, neighbours, substeps, moves):
    f32 = jnp.float32
    lying = populations.reshape(4, 19, 32, 128).transpose(1, 2, 0, 3).reshape(19, 128, 128)
    vmem, smem = pl.BlockSpec(memory_space=pltpu.VMEM), pl.BlockSpec(memory_space=pltpu.SMEM)
    whole = pl.BlockSpec(memory_space=pl.ANY)
    shapes = (jax.ShapeDtypeStruct((19, 128, 128), f32), jax.ShapeDtypeStruct((4,), jnp.int32))
    result, ids = pl.pallas_call(
        functools.partial(kernel, sizes),
        out_shape=(pltpu.VMEM((19, 128, 128), f32), shapes[1]),
        in_specs=[pl.BlockSpec(memory_space=pltpu.HBM)] * 4,
        out_specs=(vmem, smem),
        scratch_shapes=[
            pltpu.VMEM((19, 128, 128), f32),
            pltpu.SMEM((4, 6), jnp.int32),
            pltpu.SMEM((4,), jnp.int32),
            pltpu.SMEM((1, 2), jnp.int32),
            pltpu.SMEM((2, 4), jnp.int32),
            pltpu.SMEM((2, 4), jnp.int32),
            pltpu.VMEM((4, 4, 19, 32, 128), f32),
            pltpu.VMEM((4, 19, 48, 128), f32),
            pltpu.VMEM((12, SENT_ROWS, 128), f32),
            pltpu.VMEM((2, 19, 32, 128), f32),
            pltpu.VMEM((2, SENT_ROWS, 128), f32),
            pltpu.VMEM((4, 19, 32, 128), f32),
            pltpu.VMEM((4, SENT_ROWS, 128), f32),
            pltpu.VMEM((PLANE_ROWS, 128), f32),
            pltpu.VMEM((8, 128), f32),
            pltpu.VMEM((4, 2, 19, 48, 128), f32),
            pltpu.VMEM((19, 32, 128), f32),
            pltpu.SemaphoreType.DMA((4,)),
            pltpu.SemaphoreType.DMA((13,)),
            pltpu.SemaphoreType.DMA((13,)),
            pltpu.SemaphoreType.REGULAR,
            pltpu.SemaphoreType.REGULAR,
            pltpu.SemaphoreType.REGULAR,
        ],
        compiler_params=pltpu.CompilerParams(
            collective_id=0, has_side_effects=True, vmem_limit_bytes=53500 * 1024
        ),
        name="lattice_step",
    )(*[pltpu.with_memory_space_constraint(value, pltpu.HBM) for value in (lying, neighbours, substeps, moves)])
    result, ids = pl.pallas_call(
        write,
        out_shape=shapes,
        in_specs=[vmem, whole],
        out_specs=(whole, whole),
        scratch_shapes=[pltpu.SemaphoreType.DMA((5,))],
        compiler_params=pltpu.CompilerParams(vmem_limit_bytes=36 * 1024 * 1024),
        name="write_out",
    )(result, ids)
    return result.reshape(19, 32, 4, 128).transpose(2, 0, 1, 3).reshape(4, 19, 4096), ids


def solution(mesh):
    sizes = (mesh.shape["gy"], mesh.shape["gz"], mesh.size)
    return jax.shard_map(
        functools.partial(shards, sizes),
        mesh=mesh,
        in_specs=(P(AXES, None, None), P(AXES, None), P(AXES), P(AXES, None)),
        out_specs=(P(AXES, None, None), P(AXES)),
        check_vma=False,
    )
```

```python
import functools

import jax
import jax.numpy as jnp
import numpy as np
from jax import lax
from jax.experimental import pallas as pl
from jax.experimental.pallas import tpu as pltpu
from jax.sharding import PartitionSpec as P

MESH = pl.DeviceIdType.MESH
AXES = ("gx", "gy", "gz")
VELOCITY = [
    (0, 0, 0), (1, 0, 0), (-1, 0, 0), (0, 1, 0), (0, -1, 0), (0, 0, 1), (0, 0, -1),
    (1, 1, 0), (-1, -1, 0), (1, -1, 0), (-1, 1, 0), (1, 0, 1), (-1, 0, -1),
    (1, 0, -1), (-1, 0, 1), (0, 1, 1), (0, -1, -1), (0, 1, -1), (0, -1, 1),
]
OPPOSITE = [0, 2, 1, 4, 3, 6, 5, 8, 7, 10, 9, 12, 11, 14, 13, 16, 15, 18, 17]
LEAVING = [
    [2, 8, 10, 12, 14], [1, 7, 9, 11, 13], [4, 8, 9, 16, 18],
    [3, 7, 10, 15, 17], [6, 12, 13, 16, 17], [5, 11, 14, 15, 18],
]
Y_SENT, Z_SENT, X_SENT, SENT_ROWS = 0, 24, 48, 64
X_ROW, Y_ROW, Z_ROW, PLANE_ROWS = 0, 24, 56, 96
TOP = 8


def turned(value, by):
    by = by % 128
    return value if by == 0 else pltpu.roll(value, by, 1)


def grid_iotas():
    row = lax.broadcasted_iota(jnp.int32, (8, 128), 0)
    lane = lax.broadcasted_iota(jnp.int32, (8, 128), 1)
    return row, lane


def unpacked(raw, cube, block):
    for q in range(19):
        for v in range(4):
            cube[block, q, TOP + 8 * v : TOP + 8 * v + 8, :] = raw[q, pl.ds(32 * v + block, 8, stride=4), :]


def pack_faces(cube, packets, block, slot, corner):
    row, lane = grid_iotas()
    even = row % 2 == 0
    place = (lane // 16 - row % 2) % 8
    for face in range(2):
        start = TOP if face == 0 else TOP + 30
        for k in range(5):
            at = 10 * face + 2 * k
            pair = cube[block, LEAVING[face][k], start : start + 2, :]
            if at < 16:
                packets[slot, X_SENT + at : X_SENT + at + 2, :] = pair
            else:
                corner[at - 16 : at - 14, :] = pair
                corner[at - 12 : at - 10, :] = pair
    ys, zs = [], []
    for v in range(4):
        base = TOP + 8 * v
        kept = jnp.zeros((8, 128), jnp.float32)
        for k in range(5):
            far = cube[block, LEAVING[3][k], base + 1 : base + 9, :]
            near = cube[block, LEAVING[2][k], base - 1 : base + 7, :]
            moved = turned(jnp.where(even, far, near), 16 * (k + 1))
            kept = jnp.where(place == k, moved, kept)
        ys.append(kept)
        kept = jnp.zeros((8, 128), jnp.float32)
        for k in range(5):
            near = cube[block, LEAVING[4][k], base : base + 8, :]
            far = cube[block, LEAVING[5][k], base : base + 8, :]
            moved = turned(jnp.where(lane % 16 == 15, far, near), 2 * k + 1)
            kept = jnp.where(lane % 16 // 2 == k, moved, kept)
        zs.append(kept)
    ys[0] = jnp.where(place >= 5, turned(ys[3], 80), ys[0])
    ys[1] = jnp.where(place >= 5, turned(ys[3], 32), ys[1])
    zs[0] = jnp.where(lane % 16 >= 10, turned(zs[3], 10), zs[0])
    zs[1] = jnp.where(lane % 16 >= 10, turned(zs[3], 4), zs[1])
    rest = corner[...]
    rest = jnp.where(row < 4, rest, turned(rest, 64))
    ys[1] = jnp.where(place == 7, jnp.where(even, turned(rest, 64), turned(rest, 80)), ys[1])
    ys[2] = jnp.where(place >= 5, jnp.where(even, turned(rest, 80), turned(rest, 96)), ys[2])
    for v in range(3):
        packets[slot, Y_SENT + 8 * v : Y_SENT + 8 * v + 8, :] = ys[v]
        packets[slot, Z_SENT + 8 * v : Z_SENT + 8 * v + 8, :] = zs[v]


def spread(sent, slot, planes):
    row, lane = grid_iotas()
    place = (lane // 16 - row % 2) % 8
    ys = [sent[slot, Y_SENT + 8 * v : Y_SENT + 8 * v + 8, :] for v in range(3)]
    zs = [sent[slot, Z_SENT + 8 * v : Z_SENT + 8 * v + 8, :] for v in range(3)]
    ys.append(jnp.where(place < 3, turned(ys[0], -80), turned(ys[1], -32)))
    zs.append(jnp.where(lane % 16 < 6, turned(zs[0], -10), turned(zs[1], -4)))
    for v in range(4):
        planes[Y_ROW + 8 * v : Y_ROW + 8 * v + 8, :] = ys[v]
        planes[Z_ROW + 8 * v : Z_ROW + 8 * v + 8, :] = zs[v]
    for v in range(2):
        planes[X_ROW + 8 * v : X_ROW + 8 * v + 8, :] = sent[slot, X_SENT + 8 * v : X_SENT + 8 * v + 8, :]
    even = row % 2 == 0
    one = jnp.where(even, turned(ys[1], -64), turned(ys[1], -80))
    rest = jnp.where(lane // 16 == 3, one, jnp.where(even, turned(ys[2], -80), turned(ys[2], -96)))
    planes[X_ROW + 16 : X_ROW + 24, :] = rest
    below = turned(planes[X_ROW + 20 : X_ROW + 28, :], 64)
    planes[X_ROW + 16 : X_ROW + 20, :] = jnp.where(lane < 64, rest, below)[0:4]


def assemble(packets, nbr, block, first, out, slot):
    row, lane = grid_iotas()
    at, valid = [], []
    for face in range(6):
        near = nbr[block, face]
        valid.append(jnp.full((8, 128), near, jnp.int32) >= 0)
        at.append(jnp.clip(near - first, 0, 11))
    place = (lane // 16 - row % 2) % 8
    upper, lower = slice(X_SENT, X_SENT + 8), slice(X_SENT + 8, X_SENT + 16)
    out[slot, upper, :] = jnp.where(valid[1], packets[at[1], upper, :], -1.0)
    second = jnp.where(valid[1], packets[at[1], lower, :], -1.0)
    out[slot, lower, :] = jnp.where(row < 2, second, jnp.where(valid[0], packets[at[0], lower, :], -1.0))
    for v in range(3):
        rows = slice(Y_SENT + 8 * v, Y_SENT + 8 * v + 8)
        even_rows = jnp.where(valid[2], packets[at[2], rows, :], -1.0)
        odd_rows = jnp.where(valid[3], packets[at[3], rows, :], -1.0)
        value = jnp.where(row % 2 == 0, even_rows, odd_rows)
        if v > 0:
            value = jnp.where(place >= (7 if v == 1 else 5), jnp.where(valid[0], packets[at[0], rows, :], -1.0), value)
        out[slot, rows, :] = value
        rows = slice(Z_SENT + 8 * v, Z_SENT + 8 * v + 8)
        low = jnp.where(valid[4], packets[at[4], rows, :], -1.0)
        high = jnp.where(valid[5], packets[at[5], rows, :], -1.0)
        out[slot, rows, :] = jnp.where(lane % 2 == 0, low, high)


def outside(which, v):
    row, lane = grid_iotas()
    cx, cy, cz = VELOCITY[which]
    x_mask = y_mask = z_mask = None
    if cx == 1 and v == 0:
        x_mask = row < 2
    if cx == -1 and v == 3:
        x_mask = row >= 6
    if cy == 1:
        y_mask = (row % 2 == 0) & (lane < 16)
    if cy == -1:
        y_mask = (row % 2 == 1) & (lane >= 112)
    if cz == 1:
        z_mask = lane % 16 == 0
    if cz == -1:
        z_mask = lane % 16 == 15
    return x_mask, y_mask, z_mask


def build_halo(planes, halo):
    row, lane = grid_iotas()
    for which in range(1, 19):
        cx, cy, cz = VELOCITY[which]
        for v in range(4):
            x_mask, y_mask, z_mask = outside(which, v)
            value = None
            if z_mask is not None:
                face = 4 if cz == 1 else 5
                k = LEAVING[face ^ 1].index(which)
                by = 16 * cy - (2 * k + 1) + (-15 if cz == 1 else 15)
                start = Z_ROW + 8 * v - 2 * cx
                value = planes[start : start + 8, :]
                if cy != 0:
                    beside = planes[start - cy : start - cy + 8, :]
                    to = (lane + by) % 128
                    value = jnp.where(to < 16 if cy == 1 else to >= 112, beside, value)
                value = turned(value, by)
            if y_mask is not None:
                face = 2 if cy == 1 else 3
                k = LEAVING[face ^ 1].index(which)
                by = -16 * k if cy == 1 else 112 - 16 * (k + 1)
                start = Y_ROW + 8 * v - 2 * cx
                plane = planes[start : start + 8, :]
                line = turned(plane, by)
                if cz != 0:
                    line = jnp.where(lane % 16 == (0 if cz == 1 else 15), line, turned(plane, by + cz))
                value = line if value is None else jnp.where(y_mask, line, value)
            if x_mask is not None:
                face = 0 if cx == 1 else 1
                k = LEAVING[face ^ 1].index(which)
                at = X_ROW + 10 * (face ^ 1) + 2 * k
                pair = planes[at : at + 2, :]
                upper, lower = pair[0:1], pair[1:2]
                if cy == 1:
                    high, low = turned(upper, 16), turned(lower, 16)
                    lane1 = lane[0:1]
                    lower = jnp.where(lane1 < 16, high, low)
                    upper = jnp.where(lane1 < 16, upper, high)
                elif cy == -1:
                    high, low = turned(upper, -16), turned(lower, -16)
                    lane1 = lane[0:1]
                    upper = jnp.where(lane1 >= 112, low, high)
                    lower = jnp.where(lane1 >= 112, lower, low)
                elif cz != 0:
                    edge = lane[0:1] % 16 == (0 if cz == 1 else 15)
                    upper = jnp.where(edge, upper, turned(upper, cz))
                    lower = jnp.where(edge, lower, turned(lower, cz))
                both = jnp.where(
                    row % 2 == 0,
                    jnp.broadcast_to(upper, (8, 128)),
                    jnp.broadcast_to(lower, (8, 128)),
                )
                value = both if value is None else jnp.where(x_mask, both, value)
            if value is not None:
                halo[which, 8 * v : 8 * v + 8, :] = value


def collide(f, shear):
    s = {q: f[q] + f[q + 1] for q in range(1, 19, 2)}
    d = {q: f[q] - f[q + 1] for q in range(1, 19, 2)}
    sx, sy, sz = s[1], s[3], s[5]
    sxy, sxz, syz = s[7] + s[9], s[11] + s[13], s[15] + s[17]
    along = sx + (sy + sz)
    across = sxy + (sxz + syz)
    xa, xb = d[7] + d[9], d[11] + d[13]
    ya, yb = d[15] + d[17], d[7] - d[9]
    za, zb = d[11] - d[13], d[15] - d[17]
    x_sum, y_sum, z_sum = xa + xb, ya + yb, za + zb
    jx, jy, jz = d[1] + x_sum, d[3] + y_sum, d[5] + z_sum
    xx, yy, zz = jx * jx, jy * jy, jz * jz
    yz_sum = yy + zz
    jj = xx + yz_sum
    e1 = (1.19 * 19.0 / 2394.0) * ((across - f[0]) - jj)
    e2 = (1.4 / 252.0) * ((9.0 * f[0] - 7.0 * along) - (2.0 * across - 5.5 * jj))
    qx = (1.2 / 40.0 * 5.0 / 3.0) * (x_sum - 2.0 * d[1])
    qy = (1.2 / 40.0 * 5.0 / 3.0) * (y_sum - 2.0 * d[3])
    qz = (1.2 / 40.0 * 5.0 / 3.0) * (z_sum - 2.0 * d[5])
    axial = (2.0 * sx) - (sy + sz)
    planar = (sxy + sxz) - 2.0 * syz
    stress = 2.0 * xx - yz_sum
    e9 = (shear * (1.0 / 36.0)) * ((axial + planar) - stress)
    e10 = (1.4 / 72.0) * ((planar - 2.0 * axial) + 0.5 * stress)
    axial_w = sy - sz
    planar_w = sxy - sxz
    stress_w = yy - zz
    e11 = (shear * (1.0 / 12.0)) * ((axial_w + planar_w) - stress_w)
    e12 = (1.4 / 24.0) * ((planar_w - 2.0 * axial_w) + 0.5 * stress_w)
    quarter = shear * 0.25
    e13 = quarter * ((s[7] - s[9]) - jx * jy)
    e14 = quarter * ((s[15] - s[17]) - jy * jz)
    e15 = quarter * ((s[11] - s[13]) - jx * jz)
    e16 = (1.98 / 8.0) * (xa - xb)
    e17 = (1.98 / 8.0) * (ya - yb)
    e18 = (1.98 / 8.0) * (za - zb)
    post = [None] * 19
    post[0] = f[0] + (30.0 * e1 - 12.0 * e2)
    base = 11.0 * e1 + 4.0 * e2
    t9 = e9 - 2.0 * e10
    t11 = e11 - 2.0 * e12
    evens = {1: 2.0 * t9 - base, 3: t11 - (t9 + base), 5: -((t11 + t9) + base)}
    base = 8.0 * e1 + e2
    u9 = e9 + e10
    u11 = e11 + e12
    upper, lower, third = base + u9 + u11, base + u9 - u11, base - 2.0 * u9
    evens.update({7: upper + e13, 9: upper - e13, 11: lower + e15, 13: lower - e15, 15: third + e14, 17: third - e14})
    xp, xm = qx + e16, qx - e16
    yp, ym = qy + e17, qy - e17
    zp, zm = qz + e18, qz - e18
    odds = {
        1: -4.0 * qx, 3: -4.0 * qy, 5: -4.0 * qz,
        7: xp + ym, 9: xp - ym, 11: xm + zp, 13: xm - zp, 15: yp + zm, 17: yp - zm,
    }
    for q in range(1, 19, 2):
        post[q] = f[q] - (evens[q] + odds[q])
        post[q + 1] = f[q + 1] - (evens[q] - odds[q])
    return post


def arrived(q, v, post, halo):
    _, lane = grid_iotas()
    cx, cy, cz = VELOCITY[q]
    start = TOP + 8 * v - 2 * cx
    value = post[q, start : start + 8, :]
    by = 16 * cy + cz
    if cy != 0:
        beside = post[q, start - cy : start - cy + 8, :]
        value = jnp.where(lane >= 128 - by if cy == 1 else lane < -by, beside, value)
    value = turned(value, by)
    masks = [m for m in outside(q, v) if m is not None]
    if masks:
        edge = halo[q, 8 * v : 8 * v + 8, :]
        bounced = post[OPPOSITE[q], TOP + 8 * v : TOP + 8 * v + 8, :]
        value = jnp.where(functools.reduce(jnp.logical_or, masks), jnp.where(edge < 0.0, bounced, edge), value)
    return value


def collide_first(first, post, shear):
    for v in range(4):
        values = collide([first[q, 8 * v : 8 * v + 8, :] for q in range(19)], shear)
        for q in range(19):
            post[q, TOP + 8 * v : TOP + 8 * v + 8, :] = values[q]


def run_and_collide(state, post, target, halo, shear):
    for v in range(4):
        values = [arrived(q, v, post, halo) for q in range(19)]
        for q in range(19):
            state[q, 8 * v : 8 * v + 8, :] = values[q]
        values = collide(values, shear)
        for q in range(19):
            target[q, TOP + 8 * v : TOP + 8 * v + 8, :] = values[q]


def run_last(state, post, halo):
    for v in range(4):
        for q in range(19):
            state[q, 8 * v : 8 * v + 8, :] = arrived(q, v, post, halo)


def kernel(
    sizes, pop, nbr_in, sub_in, moves_in, out, ids, raw, nbr, sub, moves, mine, theirs, state, cube, packets, gone, interface_out, first, interface, planes, corner, post, halo,
    load_sem, send_sem, recv_sem, answer_sem, near_sem, across_sem,
):
    ny, nz, total = sizes
    bit = ny * nz
    me = lax.axis_index("gx") * bit + lax.axis_index("gy") * nz + lax.axis_index("gz")

    def place(d):
        return (d // bit, d // nz % ny, d % nz)

    partner_id = lax.rem(me // bit, 2) * (-2 * bit) + bit + me
    partner = place(partner_id)
    later = place(lax.rem(me + 1, total))
    before = place(lax.rem(me + total - 1, total))

    loads = [
        pltpu.make_async_copy(source, target, load_sem.at[k]) for k, (source, target) in enumerate(((pop, raw), (nbr_in, nbr), (sub_in, sub), (moves_in, moves)))
    ]
    for load in loads:
        load.start()

    greeter = lax.rem(me // bit, 2) == 0
    inner = lax.rem(me, bit)
    at_start, at_end = inner == 0, inner == bit - 1
    answerer = jnp.logical_not(greeter)
    barrier = pltpu.get_barrier_semaphore()

    def signal(semaphore, device):
        pl.semaphore_signal(semaphore, inc=1, device_id=device, device_id_type=MESH)

    @pl.when(greeter)
    def _():
        signal(barrier, partner)

    @pl.when(answerer & at_start)
    def _():
        signal(barrier, before)

    @pl.when(greeter & at_start)
    def _():
        signal(barrier, before)

    def remote(source, target, number, device):
        return pltpu.make_async_remote_copy(
            src_ref=source,
            dst_ref=target,
            send_sem=send_sem.at[number],
            recv_sem=recv_sem.at[number],
            device_id=device,
            device_id_type=MESH,
        )

    @pl.when(answerer & jnp.logical_not(at_end))
    def _():
        pl.semaphore_wait(barrier, 1)

    @pl.when(answerer & at_end)
    def _():
        pl.semaphore_wait(barrier, 2)
        signal(across_sem, later)

    @pl.when(answerer)
    def _():
        signal(answer_sem, partner)

    @pl.when(greeter)
    def _():
        pl.semaphore_wait(answer_sem, 1)

    @pl.when(greeter & jnp.logical_not(at_start))
    def _():
        signal(barrier, before)

    @pl.when(greeter & jnp.logical_not(at_end))
    def _():
        signal(barrier, later)

    gz = lax.rem(me, nz)
    z_low = lax.rem(me // nz, ny) // 2
    lowest_chips = z_low < ny // 4
    late = gz >= nz // 2

    def hear():
        @pl.when(greeter & jnp.logical_not(at_start))
        def _():
            pl.semaphore_wait(barrier, 2)

        @pl.when(greeter & at_start)
        def _():
            pl.semaphore_wait(barrier, 1)

        @pl.when(greeter)
        def _():
            signal(near_sem, partner)

        @pl.when(greeter & at_end)
        def _():
            signal(across_sem, later)


    for load in loads:
        load.wait()

    moved = [moves[0, 0], moves[0, 1]]
    for k in range(4):
        mine[0, k] = sub[k]
        mine[1, k] = moves[0, k % 2]
    orders = remote(mine, theirs, 12, partner)
    orders.start()
    blocks = [remote(gone.at[k], first.at[2 + k], k, partner) for k in range(2)]
    for k in range(2):
        for q in range(19):
            for v in range(4):
                gone[k, q, 8 * v : 8 * v + 8, :] = raw[q, pl.ds(32 * v + moved[k], 8, stride=4), :]
        blocks[k].start()

    for b in range(4):
        unpacked(raw, cube, b)

    hear()

    pack_faces(cube, packets, 0, 4, corner)

    @pl.when(answerer)
    def _():
        pl.semaphore_wait(near_sem, 1)

    @pl.when(at_start)
    def _():
        pl.semaphore_wait(across_sem, 1)

    far_later = (gz == nz // 2 - 1) | (gz == nz - 1)
    far_before = (gz == nz // 2) | (gz == 0)
    early = (far_later | far_before) & jnp.logical_not(late) & lowest_chips
    urgent = lowest_chips | at_end | jnp.logical_not(late) | (gz == nz // 2)
    halos = []
    for b in range(4):
        if b > 0:
            pack_faces(cube, packets, b, 4 + b, corner)
        for number, at, device, far in ((4 + b, b, later, far_later), (8 + b, 8 + b, before, far_before)):
            copy = remote(packets.at[4 + b], packets.at[at], number, device)
            pl.when(far & urgent)(copy.start)
            halos.append((copy, far))
    for copy, far in halos:
        pl.when(jnp.logical_not(far))(copy.start)

    low = jnp.minimum(moved[0], moved[1])
    high = jnp.maximum(moved[0], moved[1])
    stay0 = jnp.where(low > 0, 0, jnp.where(high > 1, 1, 2))
    stay1 = jnp.minimum(6 - low - high - stay0, 3)

    def keep(j, carry):
        stay = jnp.where(j == 0, stay0, stay1)

        def one(q, inner_carry):
            first[j, q] = cube[stay, q, TOP : TOP + 32, :]
            return inner_carry

        lax.fori_loop(0, 19, one, 0)
        count = jnp.full((8, 128), sub[stay], jnp.int32).astype(jnp.float32)
        collide_first(first.at[j], post.at[j, 0], 1.0 / (count * (1.0 / 1.6 - 0.5) + 0.5))
        return carry

    lax.fori_loop(0, 2, keep, 0)

    for copy, far in halos:
        pl.when(far & jnp.logical_not(urgent))(copy.start)

    orders.wait_recv()

    def shear_of(j):
        came = theirs[0, jnp.clip(theirs[1, jnp.clip(j - 2, 0, 1)], 0, 3)]
        count = jnp.where(j == 0, sub[stay0], jnp.where(j == 1, sub[stay1], came))
        return 1.0 / (jnp.full((8, 128), count, jnp.int32).astype(jnp.float32) * (1.0 / 1.6 - 0.5) + 0.5)

    def start_foreign():
        for copy in blocks:
            copy.wait_recv()

        def one(j, carry):
            collide_first(first.at[j], post.at[j, 0], shear_of(j))
            return carry

        lax.fori_loop(2, 4, one, 0)

    pl.when(early)(start_foreign)

    for copy, _ in halos:
        copy.wait_recv()

    lowest = (me - 1) * 4
    faces = []
    for k in range(2):
        assemble(packets, nbr, moved[k], lowest, interface_out, k)
        copy = remote(interface_out.at[k], interface.at[2 + k], 2 + k, partner)
        copy.start()
        faces.append(copy)

    for j, stay in enumerate((stay0, stay1)):
        assemble(packets, nbr, stay, lowest, interface, j)

    def job(j, carry):
        for k in range(2):
            @pl.when(j == 2 + k)
            def _(k=k):
                faces[k].wait_recv()

        pl.when((j == 2) & jnp.logical_not(early))(start_foreign)
        shear = shear_of(j)
        spread(interface, j, planes)
        build_halo(planes, halo)

        def one(step, inner_carry):
            now = lax.rem(step, 2)
            run_and_collide(state.at[step, j], post.at[j, now], post.at[j, 1 - now], halo, shear)
            return inner_carry

        lax.fori_loop(0, 3, one, 0)
        run_last(state.at[3, j], post.at[j, 1], halo)
        return carry

    lax.fori_loop(0, 4, job, 0)

    for s in range(4):
        here = jnp.where(moved[0] == s, 2, jnp.where(moved[1] == s, 3, jnp.where(stay0 == s, 0, 1)))
        sent = jnp.where(moved[0] == s, theirs[1, 0], theirs[1, 1])
        foreign = here >= 2
        count = jnp.where(foreign, theirs[0, jnp.clip(sent, 0, 3)], sub[s])
        step = jnp.clip(count - 1, 0, 3)
        for q in range(19):
            for v in range(4):
                out[q, pl.ds(32 * v + s, 8, stride=4), :] = state[step, here, q, 8 * v : 8 * v + 8, :]
        ids[s] = jnp.where(foreign, partner_id * 4 + sent, me * 4 + s)

    for copy in [copy for copy, _ in halos] + blocks + faces + [orders]:
        copy.wait_send()


def write(result, ids_in, out, ids, sems):
    copies = [pltpu.make_async_copy(ids_in, ids, sems.at[4])]
    for k, (low, count) in enumerate(((0, 5), (5, 5), (10, 5), (15, 4))):
        part = pl.ds(low, count)
        copies.append(pltpu.make_async_copy(result.at[part], out.at[part], sems.at[k]))
    for copy in copies:
        copy.start()
    for copy in copies:
        copy.wait()


def shards(sizes, populations, neighbours, substeps, moves):
    f32 = jnp.float32
    lying = populations.reshape(4, 19, 32, 128).transpose(1, 2, 0, 3).reshape(19, 128, 128)
    vmem, smem = pl.BlockSpec(memory_space=pltpu.VMEM), pl.BlockSpec(memory_space=pltpu.SMEM)
    whole = pl.BlockSpec(memory_space=pl.ANY)
    shapes = (jax.ShapeDtypeStruct((19, 128, 128), f32), jax.ShapeDtypeStruct((4,), jnp.int32))
    result, ids = pl.pallas_call(
        functools.partial(kernel, sizes),
        out_shape=(pltpu.VMEM((19, 128, 128), f32), shapes[1]),
        in_specs=[pl.BlockSpec(memory_space=pltpu.HBM)] * 4,
        out_specs=(vmem, smem),
        scratch_shapes=[
            pltpu.VMEM((19, 128, 128), f32),
            pltpu.SMEM((4, 6), jnp.int32),
            pltpu.SMEM((4,), jnp.int32),
            pltpu.SMEM((1, 2), jnp.int32),
            pltpu.SMEM((2, 4), jnp.int32),
            pltpu.SMEM((2, 4), jnp.int32),
            pltpu.VMEM((4, 4, 19, 32, 128), f32),
            pltpu.VMEM((4, 19, 48, 128), f32),
            pltpu.VMEM((12, SENT_ROWS, 128), f32),
            pltpu.VMEM((2, 19, 32, 128), f32),
            pltpu.VMEM((2, SENT_ROWS, 128), f32),
            pltpu.VMEM((4, 19, 32, 128), f32),
            pltpu.VMEM((4, SENT_ROWS, 128), f32),
            pltpu.VMEM((PLANE_ROWS, 128), f32),
            pltpu.VMEM((8, 128), f32),
            pltpu.VMEM((4, 2, 19, 48, 128), f32),
            pltpu.VMEM((19, 32, 128), f32),
            pltpu.SemaphoreType.DMA((4,)),
            pltpu.SemaphoreType.DMA((13,)),
            pltpu.SemaphoreType.DMA((13,)),
            pltpu.SemaphoreType.REGULAR,
            pltpu.SemaphoreType.REGULAR,
            pltpu.SemaphoreType.REGULAR,
        ],
        compiler_params=pltpu.CompilerParams(
            collective_id=0, has_side_effects=True, vmem_limit_bytes=53500 * 1024
        ),
        name="lattice_step",
    )(*[pltpu.with_memory_space_constraint(value, pltpu.HBM) for value in (lying, neighbours, substeps, moves)])
    result, ids = pl.pallas_call(
        write,
        out_shape=shapes,
        in_specs=[vmem, whole],
        out_specs=(whole, whole),
        scratch_shapes=[pltpu.SemaphoreType.DMA((5,))],
        compiler_params=pltpu.CompilerParams(vmem_limit_bytes=36 * 1024 * 1024),
        name="write_out",
    )(result, ids)
    return result.reshape(19, 32, 4, 128).transpose(2, 0, 1, 3).reshape(4, 19, 4096), ids


def solution(mesh):
    sizes = (mesh.shape["gy"], mesh.shape["gz"], mesh.size)
    return jax.shard_map(
        functools.partial(shards, sizes),
        mesh=mesh,
        in_specs=(P(AXES, None, None), P(AXES, None), P(AXES), P(AXES, None)),
        out_specs=(P(AXES, None, None), P(AXES)),
        check_vma=False,
    )
```
